32 devices in a mesh: pipe: 2 (over y), dp: 4 (over z), tensor: 4 (over x, core).
Axes of the slice: x: 2, y: 2, z: 4, core: 2. Of those that a mesh axis runs over, the one named last changes fastest.
Arguments:
- handoff: bfloat16 [2, 8192, 1024], P('pipe', 'dp', 'tensor'), may hold values from -6 to 6
- hidden_pre: bfloat16 [2, 8192, 4096], P('pipe', 'dp', 'tensor'), may hold values from -6 to 6
- down_weight: bfloat16 [2, 4096, 1024], P('pipe', 'tensor'), may hold values from -6 to 6
- up_weight: bfloat16 [2, 4096, 1024], P('pipe', 'tensor'), may hold values from -6 to 6
- moment: float32 [2, 4096, 1024], P('pipe', ('tensor', 'dp')), may hold values from -3 to 3
- second: float32 [2, 4096, 1024], P('pipe', ('tensor', 'dp')), may hold values from 0.05 to 2
Outputs:
- input_grad: bfloat16 [2, 8192, 1024], P('pipe', 'dp', 'tensor')
- new_down: bfloat16 [2, 4096, 1024], P('pipe', 'tensor')
- new_moment: float32 [2, 4096, 1024], P('pipe', ('tensor', 'dp'))
- new_second: float32 [2, 4096, 1024], P('pipe', ('tensor', 'dp'))
The draws below stay inside these ranges and needn't reach their ends.
All inputs are finite; a program needn't handle non-finite values.
Results may differ from the reference program's by a relative error of at most 0.017.
Values may be sent and summed in bfloat16 or wider, within the bound.
No kernel may reach another device: no remote copies, remote signals or barrier semaphores. Data moves between devices by JAX's collectives and lax.ppermute only.
A program may use at most 64 MiB of HBM per device.

```python
import math
import jax
import jax.numpy as jnp
from jax import lax

D = 1024
FF = 4096
TOK = 2048
PIPES = 2
HW = 1024
TOKENS = 8192
N_DP = 4
N_TENSOR = 4


def with_spikes(array, own_key, source, target, parts, factor):
    def block_of(position):
        return (jnp.arange(array.shape[position]) // (array.shape[position] // parts)).reshape((-1,) + (1,) * (array.ndim - 1 - position))

    first = jax.random.permutation(own_key, parts)[block_of(target)]
    second = (block_of(target) + parts // 2) % parts
    return jnp.where((block_of(source) == first) | (block_of(source) == second), factor * array, array)


def level_of(own_key, dims, cuts, smallest, high):
    def one(dim, blocks):
        steps = jax.random.uniform(jax.random.fold_in(jax.random.fold_in(own_key, 6), dim), (blocks,), jnp.float32, smallest / len(cuts), high / len(cuts))
        return jnp.repeat(jnp.exp(steps), dims[dim] // blocks).reshape((-1,) + (1,) * (len(dims) - dim - 1))

    gain = one(*cuts[0])
    for cut in cuts[1:]:
        gain = gain * one(*cut)
    return gain


def bell_draw(own_key, dims, width, reach, shards=(), held_as=jnp.bfloat16):
    entries = jax.random.normal(own_key, dims, jnp.float32) * width
    if len(shards) > 0:
        entries = level_of(own_key, dims, shards, -0.22, 0.18) * entries
    return jnp.clip(entries, min=-reach, max=reach).astype(held_as)


def gaussian_with(stream_key, dims, deviation, bound, cuts, heavy, held_as=jnp.bfloat16):
    entries = deviation * jax.random.normal(stream_key, dims, jnp.float32)
    if cuts:
        entries = entries * level_of(stream_key, dims, cuts, -0.22, 0.18)
    return jnp.clip(with_spikes(entries, jax.random.fold_in(stream_key, 3), *heavy), -bound, bound).astype(held_as)


def setup_inputs(seed: int = 0) -> dict:
    keys = jax.random.split(jax.random.key(seed), 7)
    handoff = bell_draw(keys[0], (PIPES, TOKENS, D), 1.0, 6.0, ((0, 2), (1, 4), (2, 4)))
    hidden_pre = gaussian_with(keys[1], (PIPES, TOKENS, FF), 1.0, 6.0, ((0, 2), (1, 4), (2, 4)), (1, 2, 4, 2.0))
    down_weight = bell_draw(keys[2], (PIPES, FF, D), 1.0, 6.0, ((0, 2), (1, 4)))
    up_weight = bell_draw(keys[3], (PIPES, FF, D), 1.0, 6.0, ((0, 2), (1, 4)))
    moment = bell_draw(keys[4], (PIPES, FF, D), 0.5, 3.0, ((0, 2), (1, 16)), jnp.float32)
    second = jnp.clip(jnp.exp(math.log(2.0) - 3.6888794 * jax.random.uniform(keys[5], (PIPES, FF, D), jnp.float32) ** level_of(keys[5], (PIPES, FF, D), ((0, 2), (1, 16)), -0.2, 0.2)), 0.05, 2.0)
    return {"handoff": handoff, "hidden_pre": hidden_pre, "down_weight": down_weight, "up_weight": up_weight, "moment": moment, "second": second}


def normal_cdf(inputs):
    return 0.5 * (1.0 + jax.scipy.special.erf(inputs * (1.0 / math.sqrt(2.0))))

def gelu_value(inputs):
    return inputs * normal_cdf(inputs)

def gelu_slope(inputs):
    return normal_cdf(inputs) + inputs * jnp.exp(-0.5 * inputs * inputs) * (1.0 / math.sqrt(2.0 * math.pi))

def reference(handoff, hidden_pre, down_weight, up_weight, moment, second):
    grads_out = []
    downs_out = []
    moments_out = []
    seconds_out = []
    for section_index in range(PIPES):
        incoming = handoff[(section_index + 1) % PIPES]
        pre_values = hidden_pre[section_index].astype(jnp.float32)
        hidden = gelu_value(pre_values).astype(jnp.bfloat16)
        down_back = jnp.dot(incoming, down_weight[section_index].T, preferred_element_type=jnp.float32)
        act_grad = (down_back * (1.0 / math.sqrt(D)) * gelu_slope(pre_values)).astype(jnp.bfloat16)
        running = jnp.zeros((TOKENS, D), jnp.float32)
        for tensor_rank in range(N_TENSOR):
            lower = tensor_rank * HW
            partial_value = jnp.dot(act_grad[:, lower:lower + HW], up_weight[section_index][lower:lower + HW], preferred_element_type=jnp.float32)
            partial_value = lax.optimization_barrier((partial_value * (1.0 / math.sqrt(FF))).astype(jnp.bfloat16))
            running = running + partial_value.astype(jnp.float32)
        grads_out.append(running.astype(jnp.bfloat16))

        def add_term(accum, block_index):
            hidden_rows = lax.dynamic_slice_in_dim(hidden, (block_index * TOK).astype(jnp.int32), TOK, 0)
            cotan_rows = lax.dynamic_slice_in_dim(incoming, (block_index * TOK).astype(jnp.int32), TOK, 0)
            block_term = jnp.dot(hidden_rows.T, cotan_rows, preferred_element_type=jnp.float32)
            block_term = lax.optimization_barrier((block_term * (1.0 / math.sqrt(TOKENS))).astype(jnp.bfloat16))
            return (accum + block_term.astype(jnp.float32), None)
        gradient, _ = lax.scan(add_term, jnp.zeros((FF, D), jnp.float32), jnp.arange(N_DP, dtype=jnp.int32))
        new_m = 0.9 * moment[section_index] + 0.1 * gradient
        new_v = 0.95 * second[section_index] + 0.05 * gradient * gradient
        fresh_rows = down_weight[section_index].astype(jnp.float32) - 0.2 * new_m / (jnp.sqrt(new_v) + 1e-08)
        downs_out.append(fresh_rows.astype(jnp.bfloat16))
        moments_out.append(new_m)
        seconds_out.append(new_v)
    return (jnp.stack(grads_out), jnp.stack(downs_out), jnp.stack(moments_out), jnp.stack(seconds_out))
```

```python
import math

import jax
import jax.numpy as jnp
from jax import lax
from jax.experimental import pallas as pl
from jax.experimental.pallas import tpu as pltpu
from jax.sharding import PartitionSpec as P

F32 = jnp.float32
BF16 = jnp.bfloat16
COL_PARTS = 2
TILE = 256
CHUNKS = (((0, 0), (1, 0)), ((0, 1), (1, 1), (2, 0), (3, 0)), ((2, 1), (3, 1)))
SUMS = ("one", "one", "one",)
GATHERS = ("two", "two", "one",)
PLAN = (
    "h0", "b00", "b10", "t0", "r0", "a0", "b01", "b20", "b30", "b11", "g0", "t1", "b21",
    "b31", "t2", "p0", "r1", "a1", "w0", "r2", "a2", "g1", "x0", "l0", "x1", "g2", "l2",
    "l1",
)
ANYWHERE = pl.BlockSpec(memory_space=pl.ANY)
TOKEN = jax.ShapeDtypeStruct((8, 128), F32)
SMALL = pl.CostEstimate(flops=1024, bytes_accessed=1024, transcendentals=0)


def from_behind(block, axis, distance):
    devices = range(lax.axis_size(axis))
    route = [((i - distance) % len(devices), i) for i in devices]
    return lax.ppermute(block, axis, route)


def normal_cdf(inputs):
    return 0.5 * (1.0 + jax.scipy.special.erf(inputs * (1.0 / math.sqrt(2.0))))


def gelu_value(inputs):
    return inputs * normal_cdf(inputs)


def gelu_slope(inputs):
    return normal_cdf(inputs) + inputs * jnp.exp(-0.5 * inputs * inputs) * (
        1.0 / math.sqrt(2.0 * math.pi)
    )


def hidden_of(hidden_pre):
    return gelu_value(hidden_pre.astype(F32)).astype(BF16)


def act_grad_of(incoming, down, hidden_pre):
    back = lax.dot_general(incoming, down, (((1,), (1,)), ((), ())), preferred_element_type=F32)
    scale = 1.0 / math.sqrt(down.shape[1])
    return (back * scale * gelu_slope(hidden_pre.astype(F32))).astype(BF16)


def term_of(hidden, columns, token_total):
    product = lax.dot_general(
        hidden, columns, (((0,), (0,)), ((), ())), preferred_element_type=F32
    )
    return (product * (1.0 / math.sqrt(token_total))).astype(BF16)


def adam(gradient, moment, second, rows):
    new_m = 0.9 * moment + 0.1 * gradient
    new_v = 0.95 * second + 0.05 * gradient * gradient
    fresh = (rows.astype(F32) - 0.2 * new_m / (jnp.sqrt(new_v) + 1e-08)).astype(BF16)
    return new_m, new_v, fresh


def plain(handoff, hidden_pre, down_weight, up_weight, moment, second):
    arrived = from_behind(handoff, "pipe", -1)
    incoming = lax.all_gather(arrived, "tensor", axis=2, tiled=True)[0]
    model_width = incoming.shape[1]
    shard_rows = moment.shape[1]
    hidden_total = down_weight.shape[1] * lax.axis_size("tensor")
    token_total = incoming.shape[0] * lax.axis_size("dp")
    hidden = hidden_of(hidden_pre[0])
    act_grad = act_grad_of(incoming, down_weight[0], hidden_pre[0])
    partial_value = jnp.dot(act_grad, up_weight[0], preferred_element_type=F32) * (
        1.0 / math.sqrt(hidden_total)
    )
    input_grad = lax.psum_scatter(
        partial_value.astype(BF16), "tensor", scatter_dimension=1, tiled=True
    )
    gradient = lax.psum_scatter(
        term_of(hidden, incoming, token_total), "dp", scatter_dimension=0, tiled=True
    ).astype(F32)
    own_rows = lax.dynamic_slice_in_dim(
        down_weight[0], lax.axis_index("dp") * shard_rows, shard_rows, 0
    )
    new_m, new_v, fresh = adam(gradient, moment[0], second[0], own_rows)
    new_down = lax.all_gather(fresh, "dp", axis=0, tiled=True)
    return (input_grad[None], new_down[None], new_m[None], new_v[None])


def params(mib):
    return pltpu.CompilerParams(vmem_limit_bytes=mib * 2**20)


def prepare(hidden_pre, model_width):
    tokens, units = hidden_pre.shape
    scale = 1.0 / math.sqrt(model_width)

    def kernel(pre_ref, hidden_ref, slope_ref, token_ref):
        token_ref[...] = jnp.zeros_like(token_ref)
        pre = pre_ref[...].astype(F32)
        phi = 0.5 * (1.0 + lax.erf(pre * (1.0 / math.sqrt(2.0))))
        hidden_ref[...] = (pre * phi).astype(BF16).T
        bell = jnp.exp(-0.5 * pre * pre) * (1.0 / math.sqrt(2.0 * math.pi))
        slope_ref[...] = ((phi + pre * bell) * scale).astype(BF16)

    return pl.pallas_call(
        kernel,
        grid=(tokens // TILE,),
        in_specs=[pl.BlockSpec((TILE, units), lambda i: (i, 0))],
        out_specs=[
            pl.BlockSpec((units, TILE), lambda i: (0, i)),
            pl.BlockSpec((TILE, units), lambda i: (i, 0)),
            pl.BlockSpec((8, 128), lambda i: (0, 0)),
        ],
        out_shape=[
            jax.ShapeDtypeStruct((units, tokens), BF16),
            jax.ShapeDtypeStruct((tokens, units), BF16),
            TOKEN,
        ],
        compiler_params=params(8),
        cost_estimate=SMALL,
        name="prepare",
    )(hidden_pre)


def terms(hidden_t, pieces, places, scale, paired, after):
    units, tokens = hidden_t.shape
    size, width = units // 4, pieces[0].shape[1]
    count, wide = len(pieces), len(pieces) * pieces[0].shape[1]
    heights = [size, size, 2 * size] if paired else [size] * 4
    number = len(heights)

    def kernel(places_ref, hidden_ref, *refs):
        piece_refs, refs = refs[:count], refs[count + len(after) :]
        out_refs, token_ref, joined = refs[:number], refs[number], refs[number + 1]
        step = pl.program_id(0)

        @pl.when(step == 0)
        def _():
            token_ref[...] = jnp.zeros_like(token_ref)
            for j in range(count):
                joined[:, j * width : (j + 1) * width] = piece_refs[j][...]

        product = jnp.dot(hidden_ref[...], joined[...], preferred_element_type=F32)
        product = (product * scale).astype(BF16)
        for j in range(4):
            @pl.when(step == j)
            def _(j=j):
                if paired and j >= 2:
                    out_refs[2][(j - 2) * size : (j - 1) * size, :] = product
                else:
                    out_refs[j][...] = product

    return pl.pallas_call(
        kernel,
        grid_spec=pltpu.PrefetchScalarGridSpec(
            num_scalar_prefetch=1,
            grid=(4,),
            in_specs=[pl.BlockSpec((size, tokens), lambda i, places: (places[i], 0))]
            + [pl.BlockSpec((tokens, width), lambda i, places: (0, 0))] * count
            + [ANYWHERE] * len(after),
            out_specs=[pl.BlockSpec((height, wide), lambda i, places: (0, 0)) for height in heights]
            + [pl.BlockSpec((8, 128), lambda i, places: (0, 0))],
            scratch_shapes=[pltpu.VMEM((tokens, wide), BF16)],
        ),
        out_shape=[jax.ShapeDtypeStruct((height, wide), BF16) for height in heights] + [TOKEN],
        compiler_params=params(16),
        cost_estimate=SMALL,
        name="terms",
    )(places, hidden_t, *pieces, *after)


def adam_chunk(shares, near, moment, second, down, columns, rank, previous, width, after):
    size, wide = shares[0].shape
    count = wide // width
    total = moment.shape[1]
    number = len(shares) + len(near)

    def kernel(columns_ref, rank_ref, *refs):
        m_ref, v_ref, down_ref = refs[number : number + 3]
        fresh_ref, new_m_ref, new_v_ref, token_ref = refs[-4:]
        token_ref[...] = jnp.zeros_like(token_ref)
        gradient = refs[0][...].astype(F32)
        for ref in refs[1:number]:
            gradient += ref[...].astype(F32)
        new_m = 0.9 * m_ref[...] + 0.1 * gradient
        new_v = 0.95 * v_ref[...] + 0.05 * gradient * gradient
        new_m_ref[...] = new_m
        new_v_ref[...] = new_v
        rows = down_ref[...].astype(F32)
        fresh_ref[...] = (rows - 0.2 * new_m / (jnp.sqrt(new_v) + 1e-08)).astype(BF16)

    here = pl.BlockSpec((size, width), lambda j, columns, rank: (0, j))
    below = pl.BlockSpec((size, width), lambda j, columns, rank: (1, j))
    there = pl.BlockSpec((size, width), lambda j, columns, rank: (0, columns[j]))
    return pl.pallas_call(
        kernel,
        grid_spec=pltpu.PrefetchScalarGridSpec(
            num_scalar_prefetch=2,
            grid=(count,),
            in_specs=[here] * len(shares)
            + [below] * len(near)
            + [there] * 2
            + [pl.BlockSpec((size, width), lambda j, columns, rank: (rank[0], columns[j]))]
            + [ANYWHERE] * (len(after) + len(previous)),
            out_specs=[here, there, there, pl.BlockSpec((8, 128), lambda j, columns, rank: (0, 0))],
        ),
        out_shape=[
            jax.ShapeDtypeStruct((size, wide), BF16),
            jax.ShapeDtypeStruct((size, total), F32),
            jax.ShapeDtypeStruct((size, total), F32),
            TOKEN,
        ],
        input_output_aliases={
            number + len(after) + 5: 1, number + len(after) + 6: 2
        } if previous else {},
        compiler_params=params(8),
        cost_estimate=SMALL,
        name="adam",
    )(columns, rank, *shares, *near, moment, second, down, *after, *previous)


def place_rows(shards, rows, columns, previous, total, width, after):
    size, wide = shards[0].shape
    count = wide // width
    number = len(shards)

    def kernel(rows_ref, columns_ref, *refs):
        shard_refs, out_ref, sems = refs[:number], refs[-2], refs[-1]
        copies = []
        for k in range(number):
            for j in range(count):
                copies.append(
                    pltpu.make_async_copy(
                        shard_refs[k].at[:, pl.ds(j * width, width)],
                        out_ref.at[
                            pl.ds(pl.multiple_of(rows_ref[k] * size, size), size),
                            pl.ds(pl.multiple_of(columns_ref[j] * width, width), width),
                        ],
                        sems.at[k, j],
                    )
                )
        for copy in copies:
            copy.start()
        for copy in copies:
            copy.wait()

    return pl.pallas_call(
        kernel,
        grid_spec=pltpu.PrefetchScalarGridSpec(
            num_scalar_prefetch=2,
            grid=(1,),
            in_specs=[ANYWHERE] * (number + len(after) + len(previous)),
            out_specs=ANYWHERE,
            scratch_shapes=[pltpu.SemaphoreType.DMA((number, count))],
        ),
        out_shape=jax.ShapeDtypeStruct(total, BF16),
        input_output_aliases={2 + number + len(after): 0} if previous else {},
        compiler_params=params(8),
        cost_estimate=SMALL,
        name="place",
    )(rows, columns, *shards, *after, *previous)


def partials(pieces, where, order, slope, down, up, scale, after):
    tokens, units = slope.shape
    model_width = down.shape[1]
    width = pieces[0].shape[1]
    count = len(pieces)
    block = model_width // 4
    rows = tokens

    def kernel(where_ref, order_ref, *refs):
        piece_refs, refs = refs[:count], refs[count:]
        slope_ref, down_ref, up_ref = refs[:3]
        own_ref, other_ref, send_ref, token_ref, joined, product_ref = refs[3 + len(after) :]
        token_ref[...] = jnp.zeros_like(token_ref)
        for j in range(count):
            joined[:, pl.ds(pl.multiple_of(where_ref[j] * width, width), width)] = piece_refs[j][...]
        back = lax.dot_general(
            joined[...], down_ref[...], (((1,), (1,)), ((), ())), preferred_element_type=F32
        )
        act_grad = (back * slope_ref[...].astype(F32)).astype(BF16)
        product = jnp.dot(act_grad, up_ref[...], preferred_element_type=F32) * scale
        product_ref[...] = product.astype(BF16)

        def columns(k):
            return product_ref[:, pl.ds(pl.multiple_of(order_ref[k] * block, block), block)]

        own_ref[...] = columns(0)
        other_ref[...] = columns(1)
        send_ref[:, :block] = columns(2)
        send_ref[:, block:] = columns(3)

    return pl.pallas_call(
        kernel,
        grid_spec=pltpu.PrefetchScalarGridSpec(
            num_scalar_prefetch=2,
            grid=(rows // TILE,),
            in_specs=[pl.BlockSpec((TILE, width), lambda i, w, o: (i, 0))] * count
            + [pl.BlockSpec((TILE, units), lambda i, w, o: (i, 0))]
            + [pl.BlockSpec((units, model_width), lambda i, w, o: (0, 0))] * 2
            + [ANYWHERE] * len(after),
            out_specs=[
                pl.BlockSpec((TILE, block), lambda i, w, o: (i, 0)),
                pl.BlockSpec((TILE, block), lambda i, w, o: (i, 0)),
                pl.BlockSpec((TILE, 2 * block), lambda i, w, o: (i, 0)),
                pl.BlockSpec((8, 128), lambda i, w, o: (0, 0)),
            ],
            scratch_shapes=[
                pltpu.VMEM((TILE, model_width), BF16),
                pltpu.VMEM((TILE, model_width), BF16),
            ],
        ),
        out_shape=[
            jax.ShapeDtypeStruct((rows, block), BF16),
            jax.ShapeDtypeStruct((rows, block), BF16),
            jax.ShapeDtypeStruct((rows, 2 * block), BF16),
            TOKEN,
        ],
        compiler_params=params(20),
        cost_estimate=SMALL,
        name="partials",
    )(where, order, *pieces, slope, down, up, *after)


def on_device(handoff, hidden_pre, down_weight, up_weight, moment, second):
    rank = lax.axis_index("dp")
    tensor = lax.axis_index("tensor")
    handoff, hidden_pre, down, up = handoff[0], hidden_pre[0], down_weight[0], up_weight[0]
    tokens, block = handoff.shape
    width = block // COL_PARTS
    model_width = down.shape[1]

    def swapped(value, axis, distance):
        return lax.ppermute(value, axis, [(i, i ^ distance) for i in range(4)])

    def column_of(key):
        return (tensor ^ key[0]) * COL_PARTS + key[1]

    def columns_of(keys):
        return jnp.stack([column_of(key) for key in keys]).astype(jnp.int32)

    shards = jnp.stack([rank, rank ^ 1, rank ^ 2, rank ^ 3]).astype(jnp.int32)
    paired = jnp.stack([rank, rank ^ 2, rank ^ 3, rank ^ 1]).astype(jnp.int32)
    rank_now = rank.astype(jnp.int32)[None]
    order = jnp.stack([tensor, tensor ^ 2, tensor ^ 1, tensor ^ 3]).astype(jnp.int32)
    term_scale = 1.0 / math.sqrt(tokens * 4)
    partial_scale = 1.0 / math.sqrt(down.shape[0] * 4)
    columns = [columns_of(chunk) for chunk in CHUNKS]
    keys = [(b, g) for g in range(COL_PARTS) for b in range(4)]
    where = columns_of(keys)
    held, values, moments, new_down = [], {}, [], []

    def after():
        out = list(held)
        held.clear()
        return out

    def arrive(name):
        value, token = lax.optimization_barrier((values[name], values["token"]))
        values[name] = value
        held.extend([value, token])

    for part in range(COL_PARTS):
        columns_now = handoff[:, part * width : (part + 1) * width]
        values["b0" + str(part)] = from_behind(columns_now, "pipe", -1)

    for name in PLAN:
        kind, k = name[0], int(name[1])
        if kind == "h":
            values["hidden"], values["slope"], values["token"] = prepare(hidden_pre, model_width)
        elif kind == "b":
            arrive(name)
            part = name[2]
            if k == 0:
                values["b1" + part] = swapped(values[name], "tensor", 1)
                values["b2" + part] = swapped(values[name], "tensor", 2)
            elif k == 2:
                values["b3" + part] = swapped(values[name], "tensor", 1)
        elif kind == "t":
            pieces = [values["b%d%d" % key] for key in CHUNKS[k]]
            pair = SUMS[k] == "two"
            *out, values["token"] = terms(
                values["hidden"], pieces, paired if pair else shards, term_scale, pair, after()
            )
            if pair:
                values["s0" + name[1]], values["s2" + name[1]] = out[:2]
                values["m" + name[1]] = swapped(out[2], "dp", 1)
            else:
                values["s0" + name[1]] = out[0]
                for j in (3, 2, 1):
                    values["s%d%d" % (j, k)] = swapped(out[j], "dp", j)
        elif kind == "m":
            arrive(name)
            size = values["s0" + name[1]].shape[0]
            far = values["s2" + name[1]].astype(F32) + values[name][:size].astype(F32)
            values["s2" + name[1]] = swapped(far.astype(BF16), "dp", 2)
        elif kind == "r":
            for j in (2,) if SUMS[k] == "two" else (3, 2, 1):
                arrive("s%d%d" % (j, k))
        elif kind == "a":
            if SUMS[k] == "two":
                shares, near = [values["s%d%d" % (j, k)] for j in (0, 2)], [values["m" + name[1]]]
            else:
                shares, near = [values["s%d%d" % (j, k)] for j in range(4)], []
            fresh, *moments[:], values["token"] = adam_chunk(
                shares, near, moment[0], second[0], down, columns[k], rank_now,
                moments, width, after(),
            )
            values["g0" + name[1]] = fresh
            values["g2" + name[1]] = swapped(fresh, "dp", 2)
            values["g1" + name[1]] = swapped(fresh, "dp", 1)
            if GATHERS[k] == "one":
                values["g3" + name[1]] = swapped(fresh, "dp", 3)
        elif kind == "g":
            arrive("g2" + name[1])
            if GATHERS[k] != "one":
                values["g3" + name[1]] = swapped(values["g2" + name[1]], "dp", 1)
        elif kind == "l":
            gathered = [values["g%d%d" % (j, k)] for j in range(4)]
            new_down[:] = [
                place_rows(gathered, shards, columns[k], new_down, down.shape, width, after())
            ]
        elif kind == "p":
            pieces = [values["b%d%d" % key] for key in keys]
            values["own"], values["other"], values["x0"], values["token"] = partials(
                pieces, where, order, values["slope"], down, up, partial_scale, after()
            )
            if "w0" not in PLAN:
                values["x0"] = swapped(values["x0"], "tensor", 1)
        elif kind == "w":
            arrive("x0")
            values["x0"] = swapped(values["x0"], "tensor", 1)
        elif kind == "x" and k == 0:
            arrive("x0")
            other = values["other"].astype(F32) + values["x0"][:, block:].astype(F32)
            values["x1"] = swapped(other.astype(BF16), "tensor", 2)
        elif kind == "x":
            arrive("x1")
            own = values["own"].astype(F32) + values["x0"][:, :block].astype(F32)
            input_grad = (own + values["x1"].astype(F32)).astype(BF16)
    return (input_grad[None], new_down[0][None], moments[0][None], moments[1][None])


def solution(mesh):
    placed = (
        P("pipe", "dp", "tensor"),
        P("pipe", "dp", "tensor"),
        P("pipe", "tensor", None),
        P("pipe", "tensor", None),
        P("pipe", ("tensor", "dp"), None),
        P("pipe", ("tensor", "dp"), None),
    )
    fits = mesh.shape["tensor"] == 4 and mesh.shape["dp"] == 4
    return jax.shard_map(
        on_device if fits else plain,
        mesh=mesh,
        in_specs=placed,
        out_specs=(
            P("pipe", "dp", "tensor"),
            P("pipe", "tensor", None),
            P("pipe", ("tensor", "dp"), None),
            P("pipe", ("tensor", "dp"), None),
        ),
        check_vma=False,
    )
```

```python
import math

import jax
import jax.numpy as jnp
from jax import lax
from jax.experimental import pallas as pl
from jax.experimental.pallas import tpu as pltpu
from jax.sharding import PartitionSpec as P

F32 = jnp.float32
BF16 = jnp.bfloat16
COL_PARTS = 2
TILE = 256
CHUNKS = (((0, 0), (1, 0)), ((0, 1), (1, 1), (2, 0), (3, 0)), ((2, 1), (3, 1)))
SUMS = ("one", "one", "one",)
GATHERS = ("two", "two", "one",)
PLAN = (
    "h0", "b00", "b10", "t0", "b01", "r0", "a0", "b11", "b20", "g0", "b30", "t1", "b21",
    "b31", "t2", "p0", "r1", "l0", "a1", "w0", "r2", "a2", "g1", "x0", "g2", "x1", "l2",
    "l1",
)
ANYWHERE = pl.BlockSpec(memory_space=pl.ANY)
TOKEN = jax.ShapeDtypeStruct((8, 128), F32)
SMALL = pl.CostEstimate(flops=1024, bytes_accessed=1024, transcendentals=0)


def from_behind(block, axis, distance):
    devices = range(lax.axis_size(axis))
    route = [((i - distance) % len(devices), i) for i in devices]
    return lax.ppermute(block, axis, route)


def normal_cdf(inputs):
    return 0.5 * (1.0 + jax.scipy.special.erf(inputs * (1.0 / math.sqrt(2.0))))


def gelu_value(inputs):
    return inputs * normal_cdf(inputs)


def gelu_slope(inputs):
    return normal_cdf(inputs) + inputs * jnp.exp(-0.5 * inputs * inputs) * (
        1.0 / math.sqrt(2.0 * math.pi)
    )


def hidden_of(hidden_pre):
    return gelu_value(hidden_pre.astype(F32)).astype(BF16)


def act_grad_of(incoming, down, hidden_pre):
    back = lax.dot_general(incoming, down, (((1,), (1,)), ((), ())), preferred_element_type=F32)
    scale = 1.0 / math.sqrt(down.shape[1])
    return (back * scale * gelu_slope(hidden_pre.astype(F32))).astype(BF16)


def term_of(hidden, columns, token_total):
    product = lax.dot_general(
        hidden, columns, (((0,), (0,)), ((), ())), preferred_element_type=F32
    )
    return (product * (1.0 / math.sqrt(token_total))).astype(BF16)


def adam(gradient, moment, second, rows):
    new_m = 0.9 * moment + 0.1 * gradient
    new_v = 0.95 * second + 0.05 * gradient * gradient
    fresh = (rows.astype(F32) - 0.2 * new_m / (jnp.sqrt(new_v) + 1e-08)).astype(BF16)
    return new_m, new_v, fresh


def plain(handoff, hidden_pre, down_weight, up_weight, moment, second):
    arrived = from_behind(handoff, "pipe", -1)
    incoming = lax.all_gather(arrived, "tensor", axis=2, tiled=True)[0]
    model_width = incoming.shape[1]
    shard_rows = moment.shape[1]
    hidden_total = down_weight.shape[1] * lax.axis_size("tensor")
    token_total = incoming.shape[0] * lax.axis_size("dp")
    hidden = hidden_of(hidden_pre[0])
    act_grad = act_grad_of(incoming, down_weight[0], hidden_pre[0])
    partial_value = jnp.dot(act_grad, up_weight[0], preferred_element_type=F32) * (
        1.0 / math.sqrt(hidden_total)
    )
    input_grad = lax.psum_scatter(
        partial_value.astype(BF16), "tensor", scatter_dimension=1, tiled=True
    )
    gradient = lax.psum_scatter(
        term_of(hidden, incoming, token_total), "dp", scatter_dimension=0, tiled=True
    ).astype(F32)
    own_rows = lax.dynamic_slice_in_dim(
        down_weight[0], lax.axis_index("dp") * shard_rows, shard_rows, 0
    )
    new_m, new_v, fresh = adam(gradient, moment[0], second[0], own_rows)
    new_down = lax.all_gather(fresh, "dp", axis=0, tiled=True)
    return (input_grad[None], new_down[None], new_m[None], new_v[None])


def params(mib):
    return pltpu.CompilerParams(vmem_limit_bytes=mib * 2**20)


def prepare(hidden_pre, model_width, after):
    tokens, units = hidden_pre.shape
    scale = 1.0 / math.sqrt(model_width)

    def kernel(pre_ref, *refs):
        hidden_ref, slope_ref, token_ref = refs[len(after) :]
        token_ref[...] = jnp.zeros_like(token_ref)
        pre = pre_ref[...].astype(F32)
        phi = 0.5 * (1.0 + lax.erf(pre * (1.0 / math.sqrt(2.0))))
        hidden_ref[...] = (pre * phi).astype(BF16).T
        bell = jnp.exp(-0.5 * pre * pre) * (1.0 / math.sqrt(2.0 * math.pi))
        slope_ref[...] = ((phi + pre * bell) * scale).astype(BF16)

    return pl.pallas_call(
        kernel,
        grid=(tokens // TILE,),
        in_specs=[pl.BlockSpec((TILE, units), lambda i: (i, 0))] + [ANYWHERE] * len(after),
        out_specs=[
            pl.BlockSpec((units, TILE), lambda i: (0, i)),
            pl.BlockSpec((TILE, units), lambda i: (i, 0)),
            pl.BlockSpec((8, 128), lambda i: (0, 0)),
        ],
        out_shape=[
            jax.ShapeDtypeStruct((units, tokens), BF16),
            jax.ShapeDtypeStruct((tokens, units), BF16),
            TOKEN,
        ],
        compiler_params=params(8),
        cost_estimate=SMALL,
        name="prepare",
    )(hidden_pre, *after)


def terms(hidden_t, pieces, places, scale, paired, after):
    units, tokens = hidden_t.shape
    size, width = units // 4, pieces[0].shape[1]
    count, wide = len(pieces), len(pieces) * pieces[0].shape[1]
    heights = [size, size, 2 * size] if paired else [size] * 4
    number = len(heights)

    def kernel(places_ref, hidden_ref, *refs):
        piece_refs, refs = refs[:count], refs[count + len(after) :]
        out_refs, token_ref, joined = refs[:number], refs[number], refs[number + 1]
        step = pl.program_id(0)

        @pl.when(step == 0)
        def _():
            token_ref[...] = jnp.zeros_like(token_ref)
            for j in range(count):
                joined[:, j * width : (j + 1) * width] = piece_refs[j][...]

        product = jnp.dot(hidden_ref[...], joined[...], preferred_element_type=F32)
        product = (product * scale).astype(BF16)
        for j in range(4):
            @pl.when(step == j)
            def _(j=j):
                if paired and j >= 2:
                    out_refs[2][(j - 2) * size : (j - 1) * size, :] = product
                else:
                    out_refs[j][...] = product

    return pl.pallas_call(
        kernel,
        grid_spec=pltpu.PrefetchScalarGridSpec(
            num_scalar_prefetch=1,
            grid=(4,),
            in_specs=[pl.BlockSpec((size, tokens), lambda i, places: (places[i], 0))]
            + [pl.BlockSpec((tokens, width), lambda i, places: (0, 0))] * count
            + [ANYWHERE] * len(after),
            out_specs=[pl.BlockSpec((height, wide), lambda i, places: (0, 0)) for height in heights]
            + [pl.BlockSpec((8, 128), lambda i, places: (0, 0))],
            scratch_shapes=[pltpu.VMEM((tokens, wide), BF16)],
        ),
        out_shape=[jax.ShapeDtypeStruct((height, wide), BF16) for height in heights] + [TOKEN],
        compiler_params=params(16),
        cost_estimate=SMALL,
        name="terms",
    )(places, hidden_t, *pieces, *after)


def adam_chunk(shares, near, moment, second, down, columns, rank, previous, width, after):
    size, wide = shares[0].shape
    count = wide // width
    total = moment.shape[1]
    number = len(shares) + len(near)

    def kernel(columns_ref, rank_ref, *refs):
        m_ref, v_ref, down_ref = refs[number : number + 3]
        fresh_ref, new_m_ref, new_v_ref, token_ref = refs[-4:]
        token_ref[...] = jnp.zeros_like(token_ref)
        gradient = refs[0][...].astype(F32)
        for ref in refs[1:number]:
            gradient += ref[...].astype(F32)
        new_m = 0.9 * m_ref[...] + 0.1 * gradient
        new_v = 0.95 * v_ref[...] + 0.05 * gradient * gradient
        new_m_ref[...] = new_m
        new_v_ref[...] = new_v
        rows = down_ref[...].astype(F32)
        fresh_ref[...] = (rows - 0.2 * new_m / (jnp.sqrt(new_v) + 1e-08)).astype(BF16)

    here = pl.BlockSpec((size, width), lambda j, columns, rank: (0, j))
    below = pl.BlockSpec((size, width), lambda j, columns, rank: (1, j))
    there = pl.BlockSpec((size, width), lambda j, columns, rank: (0, columns[j]))
    return pl.pallas_call(
        kernel,
        grid_spec=pltpu.PrefetchScalarGridSpec(
            num_scalar_prefetch=2,
            grid=(count,),
            in_specs=[here] * len(shares)
            + [below] * len(near)
            + [there] * 2
            + [pl.BlockSpec((size, width), lambda j, columns, rank: (rank[0], columns[j]))]
            + [ANYWHERE] * (len(after) + len(previous)),
            out_specs=[here, there, there, pl.BlockSpec((8, 128), lambda j, columns, rank: (0, 0))],
        ),
        out_shape=[
            jax.ShapeDtypeStruct((size, wide), BF16),
            jax.ShapeDtypeStruct((size, total), F32),
            jax.ShapeDtypeStruct((size, total), F32),
            TOKEN,
        ],
        input_output_aliases={
            number + len(after) + 5: 1, number + len(after) + 6: 2
        } if previous else {},
        compiler_params=params(8),
        cost_estimate=SMALL,
        name="adam",
    )(columns, rank, *shares, *near, moment, second, down, *after, *previous)


def place_rows(shards, rows, columns, previous, total, width, after):
    size, wide = shards[0].shape
    count = wide // width
    number = len(shards)

    def kernel(rows_ref, columns_ref, *refs):
        shard_refs, out_ref, sems = refs[:number], refs[-2], refs[-1]
        copies = []
        for k in range(number):
            for j in range(count):
                copies.append(
                    pltpu.make_async_copy(
                        shard_refs[k].at[:, pl.ds(j * width, width)],
                        out_ref.at[
                            pl.ds(pl.multiple_of(rows_ref[k] * size, size), size),
                            pl.ds(pl.multiple_of(columns_ref[j] * width, width), width),
                        ],
                        sems.at[k, j],
                    )
                )
        for copy in copies:
            copy.start()
        for copy in copies:
            copy.wait()

    return pl.pallas_call(
        kernel,
        grid_spec=pltpu.PrefetchScalarGridSpec(
            num_scalar_prefetch=2,
            grid=(1,),
            in_specs=[ANYWHERE] * (number + len(after) + len(previous)),
            out_specs=ANYWHERE,
            scratch_shapes=[pltpu.SemaphoreType.DMA((number, count))],
        ),
        out_shape=jax.ShapeDtypeStruct(total, BF16),
        input_output_aliases={2 + number + len(after): 0} if previous else {},
        compiler_params=params(8),
        cost_estimate=SMALL,
        name="place",
    )(rows, columns, *shards, *after, *previous)


def partials(pieces, where, order, slope, down, up, scale, after):
    tokens, units = slope.shape
    model_width = down.shape[1]
    width = pieces[0].shape[1]
    count = len(pieces)
    block = model_width // 4
    rows = tokens

    def kernel(where_ref, order_ref, *refs):
        piece_refs, refs = refs[:count], refs[count:]
        slope_ref, down_ref, up_ref = refs[:3]
        own_ref, other_ref, send_ref, token_ref, joined, product_ref = refs[3 + len(after) :]
        token_ref[...] = jnp.zeros_like(token_ref)
        for j in range(count):
            joined[:, pl.ds(pl.multiple_of(where_ref[j] * width, width), width)] = piece_refs[j][...]
        back = lax.dot_general(
            joined[...], down_ref[...], (((1,), (1,)), ((), ())), preferred_element_type=F32
        )
        act_grad = (back * slope_ref[...].astype(F32)).astype(BF16)
        product = jnp.dot(act_grad, up_ref[...], preferred_element_type=F32) * scale
        product_ref[...] = product.astype(BF16)

        def columns(k):
            return product_ref[:, pl.ds(pl.multiple_of(order_ref[k] * block, block), block)]

        own_ref[...] = columns(0)
        other_ref[...] = columns(1)
        send_ref[:, :block] = columns(2)
        send_ref[:, block:] = columns(3)

    return pl.pallas_call(
        kernel,
        grid_spec=pltpu.PrefetchScalarGridSpec(
            num_scalar_prefetch=2,
            grid=(rows // TILE,),
            in_specs=[pl.BlockSpec((TILE, width), lambda i, w, o: (i, 0))] * count
            + [pl.BlockSpec((TILE, units), lambda i, w, o: (i, 0))]
            + [pl.BlockSpec((units, model_width), lambda i, w, o: (0, 0))] * 2
            + [ANYWHERE] * len(after),
            out_specs=[
                pl.BlockSpec((TILE, block), lambda i, w, o: (i, 0)),
                pl.BlockSpec((TILE, block), lambda i, w, o: (i, 0)),
                pl.BlockSpec((TILE, 2 * block), lambda i, w, o: (i, 0)),
                pl.BlockSpec((8, 128), lambda i, w, o: (0, 0)),
            ],
            scratch_shapes=[
                pltpu.VMEM((TILE, model_width), BF16),
                pltpu.VMEM((TILE, model_width), BF16),
            ],
        ),
        out_shape=[
            jax.ShapeDtypeStruct((rows, block), BF16),
            jax.ShapeDtypeStruct((rows, block), BF16),
            jax.ShapeDtypeStruct((rows, 2 * block), BF16),
            TOKEN,
        ],
        compiler_params=params(20),
        cost_estimate=SMALL,
        name="partials",
    )(where, order, *pieces, slope, down, up, *after)


def on_device(handoff, hidden_pre, down_weight, up_weight, moment, second):
    rank = lax.axis_index("dp")
    tensor = lax.axis_index("tensor")
    handoff, hidden_pre, down, up = handoff[0], hidden_pre[0], down_weight[0], up_weight[0]
    tokens, block = handoff.shape
    width = block // COL_PARTS
    model_width = down.shape[1]

    def swapped(value, axis, distance):
        return lax.ppermute(value, axis, [(i, i ^ distance) for i in range(4)])

    def column_of(key):
        return (tensor ^ key[0]) * COL_PARTS + key[1]

    def columns_of(keys):
        return jnp.stack([column_of(key) for key in keys]).astype(jnp.int32)

    shards = jnp.stack([rank, rank ^ 1, rank ^ 2, rank ^ 3]).astype(jnp.int32)
    paired = jnp.stack([rank, rank ^ 2, rank ^ 3, rank ^ 1]).astype(jnp.int32)
    rank_now = rank.astype(jnp.int32)[None]
    order = jnp.stack([tensor, tensor ^ 2, tensor ^ 1, tensor ^ 3]).astype(jnp.int32)
    term_scale = 1.0 / math.sqrt(tokens * 4)
    partial_scale = 1.0 / math.sqrt(down.shape[0] * 4)
    columns = [columns_of(chunk) for chunk in CHUNKS]
    keys = [(b, g) for g in range(COL_PARTS) for b in range(4)]
    where = columns_of(keys)
    held, values, moments, new_down = [], {}, [], []

    def after():
        out = list(held)
        held.clear()
        return out

    def arrive(name):
        value, token = lax.optimization_barrier((values[name], values["token"]))
        values[name] = value
        held.extend([value, token])

    for part in range(COL_PARTS):
        columns_now = handoff[:, part * width : (part + 1) * width]
        values["b0" + str(part)] = from_behind(columns_now, "pipe", -1)

    for name in PLAN:
        kind, k = name[0], int(name[1])
        if kind == "h":
            values["hidden"], values["slope"], values["token"] = prepare(
                hidden_pre, model_width, [shards, paired, rank_now, order, where, *columns]
            )
        elif kind == "b":
            arrive(name)
            part = name[2]
            if k == 0:
                values["b1" + part] = swapped(values[name], "tensor", 1)
                values["b2" + part] = swapped(values[name], "tensor", 2)
            elif k == 2:
                values["b3" + part] = swapped(values[name], "tensor", 1)
        elif kind == "t":
            pieces = [values["b%d%d" % key] for key in CHUNKS[k]]
            pair = SUMS[k] == "two"
            *out, values["token"] = terms(
                values["hidden"], pieces, paired if pair else shards, term_scale, pair, after()
            )
            if pair:
                values["s0" + name[1]], values["s2" + name[1]] = out[:2]
                values["m" + name[1]] = swapped(out[2], "dp", 1)
            else:
                values["s0" + name[1]] = out[0]
                for j in (3, 2, 1):
                    values["s%d%d" % (j, k)] = swapped(out[j], "dp", j)
        elif kind == "m":
            arrive(name)
            size = values["s0" + name[1]].shape[0]
            far = values["s2" + name[1]].astype(F32) + values[name][:size].astype(F32)
            values["s2" + name[1]] = swapped(far.astype(BF16), "dp", 2)
        elif kind == "r":
            for j in (2,) if SUMS[k] == "two" else (3, 2, 1):
                arrive("s%d%d" % (j, k))
        elif kind == "a":
            if SUMS[k] == "two":
                shares, near = [values["s%d%d" % (j, k)] for j in (0, 2)], [values["m" + name[1]]]
            else:
                shares, near = [values["s%d%d" % (j, k)] for j in range(4)], []
            fresh, *moments[:], values["token"] = adam_chunk(
                shares, near, moment[0], second[0], down, columns[k], rank_now,
                moments, width, after(),
            )
            values["g0" + name[1]] = fresh
            values["g2" + name[1]] = swapped(fresh, "dp", 2)
            values["g1" + name[1]] = swapped(fresh, "dp", 1)
            if GATHERS[k] == "one":
                values["g3" + name[1]] = swapped(fresh, "dp", 3)
        elif kind == "g":
            arrive("g2" + name[1])
            if GATHERS[k] != "one":
                values["g3" + name[1]] = swapped(values["g2" + name[1]], "dp", 1)
        elif kind == "l":
            gathered = [values["g%d%d" % (j, k)] for j in range(4)]
            new_down[:] = [
                place_rows(gathered, shards, columns[k], new_down, down.shape, width, after())
            ]
        elif kind == "p":
            pieces = [values["b%d%d" % key] for key in keys]
            values["own"], values["other"], values["x0"], values["token"] = partials(
                pieces, where, order, values["slope"], down, up, partial_scale, after()
            )
            if "w0" not in PLAN:
                values["x0"] = swapped(values["x0"], "tensor", 1)
        elif kind == "w":
            arrive("x0")
            values["x0"] = swapped(values["x0"], "tensor", 1)
        elif kind == "x" and k == 0:
            arrive("x0")
            other = values["other"].astype(F32) + values["x0"][:, block:].astype(F32)
            values["x1"] = swapped(other.astype(BF16), "tensor", 2)
        elif kind == "x":
            arrive("x1")
            own = values["own"].astype(F32) + values["x0"][:, :block].astype(F32)
            input_grad = (own + values["x1"].astype(F32)).astype(BF16)
    return (input_grad[None], new_down[0][None], moments[0][None], moments[1][None])


def solution(mesh):
    placed = (
        P("pipe", "dp", "tensor"),
        P("pipe", "dp", "tensor"),
        P("pipe", "tensor", None),
        P("pipe", "tensor", None),
        P("pipe", ("tensor", "dp"), None),
        P("pipe", ("tensor", "dp"), None),
    )
    fits = mesh.shape["tensor"] == 4 and mesh.shape["dp"] == 4
    return jax.shard_map(
        on_device if fits else plain,
        mesh=mesh,
        in_specs=placed,
        out_specs=(
            P("pipe", "dp", "tensor"),
            P("pipe", "tensor", None),
            P("pipe", ("tensor", "dp"), None),
            P("pipe", ("tensor", "dp"), None),
        ),
        check_vma=False,
    )
```

```python
import math

import jax
import jax.numpy as jnp
from jax import lax
from jax.experimental import pallas as pl
from jax.experimental.pallas import tpu as pltpu
from jax.sharding import PartitionSpec as P

F32 = jnp.float32
BF16 = jnp.bfloat16
COL_PARTS = 2
TILE = 256
CHUNKS = (((0, 0), (1, 0)), ((0, 1), (1, 1), (2, 0), (3, 0)), ((2, 1), (3, 1)))
SUMS = ("two", "one", "one",)
GATHERS = ("two", "two", "two",)
PLAN = (
    "h0", "b00", "b10", "t0", "b01", "m0", "r0", "b20", "b11", "a0", "b30", "t1", "g0",
    "e0", "b21", "b31", "t2", "p0", "r1", "a1", "r2", "x0", "a2", "e1", "g1", "e2", "g2",
    "l0", "x1", "l1", "l2",
)
ANYWHERE = pl.BlockSpec(memory_space=pl.ANY)
TOKEN = jax.ShapeDtypeStruct((8, 128), F32)
COSTS = {
    "h0": 15000000000, "t0": 10000000000, "a0": 80000000000, "t1": 40000000000,
    "t2": 6000000000, "p0": 35100000000, "a1": 6000000000, "a2": 6000000000, "l0": 4199999999,
    "l1": 1000, "l2": 80000000000,
}


def from_behind(block, axis, distance):
    devices = range(lax.axis_size(axis))
    route = [((i - distance) % len(devices), i) for i in devices]
    return lax.ppermute(block, axis, route)


def normal_cdf(inputs):
    return 0.5 * (1.0 + jax.scipy.special.erf(inputs * (1.0 / math.sqrt(2.0))))


def gelu_value(inputs):
    return inputs * normal_cdf(inputs)


def gelu_slope(inputs):
    return normal_cdf(inputs) + inputs * jnp.exp(-0.5 * inputs * inputs) * (
        1.0 / math.sqrt(2.0 * math.pi)
    )


def hidden_of(hidden_pre):
    return gelu_value(hidden_pre.astype(F32)).astype(BF16)


def act_grad_of(incoming, down, hidden_pre):
    back = lax.dot_general(incoming, down, (((1,), (1,)), ((), ())), preferred_element_type=F32)
    scale = 1.0 / math.sqrt(down.shape[1])
    return (back * scale * gelu_slope(hidden_pre.astype(F32))).astype(BF16)


def term_of(hidden, columns, token_total):
    product = lax.dot_general(
        hidden, columns, (((0,), (0,)), ((), ())), preferred_element_type=F32
    )
    return (product * (1.0 / math.sqrt(token_total))).astype(BF16)


def adam(gradient, moment, second, rows):
    new_m = 0.9 * moment + 0.1 * gradient
    new_v = 0.95 * second + 0.05 * gradient * gradient
    fresh = (rows.astype(F32) - 0.2 * new_m / (jnp.sqrt(new_v) + 1e-08)).astype(BF16)
    return new_m, new_v, fresh


def plain(handoff, hidden_pre, down_weight, up_weight, moment, second):
    arrived = from_behind(handoff, "pipe", -1)
    incoming = lax.all_gather(arrived, "tensor", axis=2, tiled=True)[0]
    model_width = incoming.shape[1]
    shard_rows = moment.shape[1]
    hidden_total = down_weight.shape[1] * lax.axis_size("tensor")
    token_total = incoming.shape[0] * lax.axis_size("dp")
    hidden = hidden_of(hidden_pre[0])
    act_grad = act_grad_of(incoming, down_weight[0], hidden_pre[0])
    partial_value = jnp.dot(act_grad, up_weight[0], preferred_element_type=F32) * (
        1.0 / math.sqrt(hidden_total)
    )
    input_grad = lax.psum_scatter(
        partial_value.astype(BF16), "tensor", scatter_dimension=1, tiled=True
    )
    gradient = lax.psum_scatter(
        term_of(hidden, incoming, token_total), "dp", scatter_dimension=0, tiled=True
    ).astype(F32)
    own_rows = lax.dynamic_slice_in_dim(
        down_weight[0], lax.axis_index("dp") * shard_rows, shard_rows, 0
    )
    new_m, new_v, fresh = adam(gradient, moment[0], second[0], own_rows)
    new_down = lax.all_gather(fresh, "dp", axis=0, tiled=True)
    return (input_grad[None], new_down[None], new_m[None], new_v[None])


def cost(item):
    return pl.CostEstimate(flops=COSTS[item], bytes_accessed=1024, transcendentals=0)


def params(mib):
    return pltpu.CompilerParams(vmem_limit_bytes=mib * 2**20)


def prepare(hidden_pre, model_width, after, item):
    tokens, units = hidden_pre.shape
    scale = 1.0 / math.sqrt(model_width)

    def kernel(pre_ref, *refs):
        hidden_ref, slope_ref, token_ref = refs[len(after) :]
        token_ref[...] = jnp.zeros_like(token_ref)
        pre = pre_ref[...].astype(F32)
        phi = 0.5 * (1.0 + lax.erf(pre * (1.0 / math.sqrt(2.0))))
        hidden_ref[...] = (pre * phi).astype(BF16).T
        bell = jnp.exp(-0.5 * pre * pre) * (1.0 / math.sqrt(2.0 * math.pi))
        slope_ref[...] = ((phi + pre * bell) * scale).astype(BF16)

    return pl.pallas_call(
        kernel,
        grid=(tokens // TILE,),
        in_specs=[pl.BlockSpec((TILE, units), lambda i: (i, 0))] + [ANYWHERE] * len(after),
        out_specs=[
            pl.BlockSpec((units, TILE), lambda i: (0, i)),
            pl.BlockSpec((TILE, units), lambda i: (i, 0)),
            pl.BlockSpec((8, 128), lambda i: (0, 0)),
        ],
        out_shape=[
            jax.ShapeDtypeStruct((units, tokens), BF16),
            jax.ShapeDtypeStruct((tokens, units), BF16),
            TOKEN,
        ],
        compiler_params=params(8),
        cost_estimate=cost(item),
        name="prepare",
    )(hidden_pre, *after)


def terms(hidden_t, pieces, places, scale, paired, after, item):
    units, tokens = hidden_t.shape
    size, width = units // 4, pieces[0].shape[1]
    count, wide = len(pieces), len(pieces) * pieces[0].shape[1]
    heights = [size, size, 2 * size] if paired else [size] * 4
    number = len(heights)

    def kernel(places_ref, hidden_ref, *refs):
        piece_refs, refs = refs[:count], refs[count + len(after) :]
        out_refs, token_ref, joined = refs[:number], refs[number], refs[number + 1]
        step = pl.program_id(0)

        @pl.when(step == 0)
        def _():
            token_ref[...] = jnp.zeros_like(token_ref)
            for j in range(count):
                joined[:, j * width : (j + 1) * width] = piece_refs[j][...]

        product = jnp.dot(hidden_ref[...], joined[...], preferred_element_type=F32)
        product = (product * scale).astype(BF16)
        for j in range(4):
            @pl.when(step == j)
            def _(j=j):
                if paired and j >= 2:
                    out_refs[2][(j - 2) * size : (j - 1) * size, :] = product
                else:
                    out_refs[j][...] = product

    return pl.pallas_call(
        kernel,
        grid_spec=pltpu.PrefetchScalarGridSpec(
            num_scalar_prefetch=1,
            grid=(4,),
            in_specs=[pl.BlockSpec((size, tokens), lambda i, places: (places[i], 0))]
            + [pl.BlockSpec((tokens, width), lambda i, places: (0, 0))] * count
            + [ANYWHERE] * len(after),
            out_specs=[pl.BlockSpec((height, wide), lambda i, places: (0, 0)) for height in heights]
            + [pl.BlockSpec((8, 128), lambda i, places: (0, 0))],
            scratch_shapes=[pltpu.VMEM((tokens, wide), BF16)],
        ),
        out_shape=[jax.ShapeDtypeStruct((height, wide), BF16) for height in heights] + [TOKEN],
        compiler_params=params(16),
        cost_estimate=cost(item),
        name="terms",
    )(places, hidden_t, *pieces, *after)


def adam_chunk(shares, near, moment, second, down, columns, rank, previous, width, after, item):
    size, wide = shares[0].shape
    count = wide // width
    total = moment.shape[1]
    number = len(shares) + len(near)

    def kernel(columns_ref, rank_ref, *refs):
        m_ref, v_ref, down_ref = refs[number : number + 3]
        fresh_ref, new_m_ref, new_v_ref, token_ref = refs[-4:]
        token_ref[...] = jnp.zeros_like(token_ref)
        gradient = refs[0][...].astype(F32)
        for ref in refs[1:number]:
            gradient += ref[...].astype(F32)
        new_m = 0.9 * m_ref[...] + 0.1 * gradient
        new_v = 0.95 * v_ref[...] + 0.05 * gradient * gradient
        new_m_ref[...] = new_m
        new_v_ref[...] = new_v
        rows = down_ref[...].astype(F32)
        fresh_ref[...] = (rows - 0.2 * new_m / (jnp.sqrt(new_v) + 1e-08)).astype(BF16)

    here = pl.BlockSpec((size, width), lambda j, columns, rank: (0, j))
    below = pl.BlockSpec((size, width), lambda j, columns, rank: (1, j))
    there = pl.BlockSpec((size, width), lambda j, columns, rank: (0, columns[j]))
    return pl.pallas_call(
        kernel,
        grid_spec=pltpu.PrefetchScalarGridSpec(
            num_scalar_prefetch=2,
            grid=(count,),
            in_specs=[here] * len(shares)
            + [below] * len(near)
            + [there] * 2
            + [pl.BlockSpec((size, width), lambda j, columns, rank: (rank[0], columns[j]))]
            + [ANYWHERE] * (len(after) + len(previous)),
            out_specs=[here, there, there, pl.BlockSpec((8, 128), lambda j, columns, rank: (0, 0))],
        ),
        out_shape=[
            jax.ShapeDtypeStruct((size, wide), BF16),
            jax.ShapeDtypeStruct((size, total), F32),
            jax.ShapeDtypeStruct((size, total), F32),
            TOKEN,
        ],
        input_output_aliases={
            number + len(after) + 5: 1, number + len(after) + 6: 2
        } if previous else {},
        compiler_params=params(8),
        cost_estimate=cost(item),
        name="adam",
    )(columns, rank, *shares, *near, moment, second, down, *after, *previous)


def place_rows(shards, rows, columns, previous, total, width, after, item):
    size, wide = shards[0].shape
    count = wide // width
    number = len(shards)

    def kernel(rows_ref, columns_ref, *refs):
        shard_refs, out_ref, token_ref, sems = refs[:number], refs[-3], refs[-2], refs[-1]
        token_ref[...] = jnp.zeros_like(token_ref)
        copies = []
        for k in range(number):
            for j in range(count):
                copies.append(
                    pltpu.make_async_copy(
                        shard_refs[k].at[:, pl.ds(j * width, width)],
                        out_ref.at[
                            pl.ds(pl.multiple_of(rows_ref[k] * size, size), size),
                            pl.ds(pl.multiple_of(columns_ref[j] * width, width), width),
                        ],
                        sems.at[k, j],
                    )
                )
        for copy in copies:
            copy.start()
        for copy in copies:
            copy.wait()

    return pl.pallas_call(
        kernel,
        grid_spec=pltpu.PrefetchScalarGridSpec(
            num_scalar_prefetch=2,
            grid=(1,),
            in_specs=[ANYWHERE] * (number + len(after) + len(previous)),
            out_specs=[ANYWHERE, pl.BlockSpec((8, 128), lambda i, rows, columns: (0, 0))],
            scratch_shapes=[pltpu.SemaphoreType.DMA((number, count))],
        ),
        out_shape=[jax.ShapeDtypeStruct(total, BF16), TOKEN],
        input_output_aliases={2 + number + len(after): 0} if previous else {},
        compiler_params=params(8),
        cost_estimate=cost(item),
        name="place",
    )(rows, columns, *shards, *after, *previous)


def partials(pieces, where, order, slope, down, up, scale, after, item):
    tokens, units = slope.shape
    model_width = down.shape[1]
    width = pieces[0].shape[1]
    count = len(pieces)
    block = model_width // 4
    rows = tokens
    step = 2 * TILE

    def kernel(where_ref, order_ref, *refs):
        piece_refs, refs = refs[:count], refs[count:]
        slope_ref, down_ref, up_ref = refs[:3]
        outs, token_ref, joined, product_ref = refs[3 + len(after) : -3], *refs[-3:]
        token_ref[...] = jnp.zeros_like(token_ref)
        for j in range(count):
            joined[:, pl.ds(pl.multiple_of(where_ref[j] * width, width), width)] = piece_refs[j][...]
        back = lax.dot_general(
            joined[...], down_ref[...], (((1,), (1,)), ((), ())), preferred_element_type=F32
        )
        act_grad = (back * slope_ref[...].astype(F32)).astype(BF16)
        product = jnp.dot(act_grad, up_ref[...], preferred_element_type=F32) * scale
        product_ref[...] = product.astype(BF16)

        for k in range(4):
            first = pl.multiple_of(order_ref[k] * block, block)
            outs[k][...] = product_ref[:, pl.ds(first, block)]

    return pl.pallas_call(
        kernel,
        grid_spec=pltpu.PrefetchScalarGridSpec(
            num_scalar_prefetch=2,
            grid=(rows // step,),
            in_specs=[pl.BlockSpec((step, width), lambda i, w, o: (i, 0))] * count
            + [pl.BlockSpec((step, units), lambda i, w, o: (i, 0))]
            + [pl.BlockSpec((units, model_width), lambda i, w, o: (0, 0))] * 2
            + [ANYWHERE] * len(after),
            out_specs=[
                pl.BlockSpec((step, block), lambda i, w, o: (i, 0)),
            ]
            * 4
            + [pl.BlockSpec((8, 128), lambda i, w, o: (0, 0))],
            scratch_shapes=[
                pltpu.VMEM((step, model_width), BF16),
                pltpu.VMEM((step, model_width), BF16),
            ],
        ),
        out_shape=[
            jax.ShapeDtypeStruct((rows, block), BF16),
        ]
        * 4
        + [TOKEN],
        compiler_params=params(28),
        cost_estimate=cost(item),
        name="partials",
    )(where, order, *pieces, slope, down, up, *after)


def on_device(handoff, hidden_pre, down_weight, up_weight, moment, second):
    rank = lax.axis_index("dp")
    tensor = lax.axis_index("tensor")
    handoff, hidden_pre, down, up = handoff[0], hidden_pre[0], down_weight[0], up_weight[0]
    tokens, block = handoff.shape
    width = block // COL_PARTS
    model_width = down.shape[1]

    def swapped(value, axis, distance):
        return lax.ppermute(value, axis, [(i, i ^ distance) for i in range(4)])

    def column_of(key):
        return (tensor ^ key[0]) * COL_PARTS + key[1]

    def columns_of(keys):
        return jnp.stack([column_of(key) for key in keys]).astype(jnp.int32)

    shards = jnp.stack([rank, rank ^ 1, rank ^ 2, rank ^ 3]).astype(jnp.int32)
    paired = jnp.stack([rank, rank ^ 2, rank ^ 3, rank ^ 1]).astype(jnp.int32)
    rank_now = rank.astype(jnp.int32)[None]
    order = jnp.stack([tensor, tensor ^ 2, tensor ^ 1, tensor ^ 3]).astype(jnp.int32)
    term_scale = 1.0 / math.sqrt(tokens * 4)
    partial_scale = 1.0 / math.sqrt(down.shape[0] * 4)
    columns = [columns_of(chunk) for chunk in CHUNKS]
    keys = [(b, g) for g in range(COL_PARTS) for b in range(4)]
    where = columns_of(keys)
    held, values, moments, new_down = [], {}, [], []

    def after():
        out = list(held)
        held.clear()
        return out

    def arrive(name):
        values[name], *held[:] = lax.optimization_barrier((values[name], values["token"], *held))
        held.append(values[name])

    for part in range(COL_PARTS):
        columns_now = handoff[:, part * width : (part + 1) * width]
        values["b0" + str(part)] = from_behind(columns_now, "pipe", -1)

    for name in PLAN:
        kind, k = name[0], int(name[1])
        if kind == "h":
            values["hidden"], values["slope"], values["token"] = prepare(
                hidden_pre, model_width, [shards, paired, rank_now, order, where, *columns],
                name,
            )
        elif kind == "b":
            arrive(name)
            part = name[2]
            if k == 0:
                values["b1" + part] = swapped(values[name], "tensor", 1)
                values["b2" + part] = swapped(values[name], "tensor", 2)
            elif k == 2:
                values["b3" + part] = swapped(values[name], "tensor", 1)
        elif kind == "t":
            pieces = [values["b%d%d" % key] for key in CHUNKS[k]]
            pair, step = SUMS[k] == "two", SUMS[k] == "tri"
            *out, values["token"] = terms(
                values["hidden"], pieces, paired if pair else shards, term_scale, pair, after(), name
            )
            if pair:
                values["s0" + name[1]], values["s2" + name[1]] = out[:2]
                values["m" + name[1]] = swapped(out[2], "dp", 1)
            else:
                values["s0" + name[1]], values["s2" + name[1]] = out[0], out[2]
                values["m" + name[1]] = swapped(out[3], "dp", 1) if step else None
                for j in (1,) if step else (3, 2, 1):
                    values["s%d%d" % (j, k)] = swapped(out[j], "dp", j)
        elif kind == "m":
            arrive(name)
            size = values["s0" + name[1]].shape[0]
            held_part = values[name][:size] if SUMS[k] == "two" else values[name]
            far = values["s2" + name[1]].astype(F32) + held_part.astype(F32)
            values["s2" + name[1]] = swapped(far.astype(BF16), "dp", 2)
        elif kind == "r":
            for j in {"two": (2,), "tri": (1, 2), "one": (3, 2, 1)}[SUMS[k]]:
                arrive("s%d%d" % (j, k))
        elif kind == "a":
            if SUMS[k] == "two":
                shares, near = [values["s%d%d" % (j, k)] for j in (0, 2)], [values["m" + name[1]]]
            else:
                number = 3 if SUMS[k] == "tri" else 4
                shares, near = [values["s%d%d" % (j, k)] for j in range(number)], []
            fresh, *moments[:], values["token"] = adam_chunk(
                shares, near, moment[0], second[0], down, columns[k], rank_now,
                moments, width, after(), name,
            )
            values["g0" + name[1]] = fresh
            values["g2" + name[1]] = swapped(fresh, "dp", 2)
            values["g1" + name[1]] = swapped(fresh, "dp", 1)
            if GATHERS[k] == "one":
                values["g3" + name[1]] = swapped(fresh, "dp", 3)
        elif kind == "g":
            arrive("g2" + name[1])
            if GATHERS[k] != "one":
                values["g3" + name[1]] = swapped(values["g2" + name[1]], "dp", 1)
        elif kind == "e":
            arrive("g1" + name[1])
        elif kind == "l":
            gathered = [values["g%d%d" % (j, k)] for j in range(4)]
            *new_down[:], values["token"] = place_rows(
                gathered, shards, columns[k], new_down, down.shape, width, after(), name
            )
        elif kind == "p":
            pieces = [values["b%d%d" % key] for key in keys]
            values["own"], values["other"], values["x2"], values["x0"], values["token"] = partials(
                pieces, where, order, values["slope"], down, up, partial_scale, after(), name
            )
            values["x2"] = swapped(values["x2"], "tensor", 1)
            if "w0" not in PLAN:
                values["x0"] = swapped(values["x0"], "tensor", 1)
        elif kind == "w":
            arrive("x0")
            values["x0"] = swapped(values["x0"], "tensor", 1)
        elif kind == "u":
            arrive("x2")
        elif kind == "x" and k == 0:
            arrive("x0")
            other = values["other"].astype(F32) + values["x0"].astype(F32)
            values["x1"] = swapped(other.astype(BF16), "tensor", 2)
        elif kind == "x":
            arrive("x1")
            own = values["own"].astype(F32) + values["x2"].astype(F32)
            input_grad = (own + values["x1"].astype(F32)).astype(BF16)
    return (input_grad[None], new_down[0][None], moments[0][None], moments[1][None])


def solution(mesh):
    placed = (
        P("pipe", "dp", "tensor"),
        P("pipe", "dp", "tensor"),
        P("pipe", "tensor", None),
        P("pipe", "tensor", None),
        P("pipe", ("tensor", "dp"), None),
        P("pipe", ("tensor", "dp"), None),
    )
    fits = mesh.shape["tensor"] == 4 and mesh.shape["dp"] == 4
    return jax.shard_map(
        on_device if fits else plain,
        mesh=mesh,
        in_specs=placed,
        out_specs=(
            P("pipe", "dp", "tensor"),
            P("pipe", "tensor", None),
            P("pipe", ("tensor", "dp"), None),
            P("pipe", ("tensor", "dp"), None),
        ),
        check_vma=False,
    )
```

```python
import math

import jax
import jax.numpy as jnp
from jax import lax
from jax.experimental import pallas as pl
from jax.experimental.pallas import tpu as pltpu
from jax.sharding import PartitionSpec as P

F32 = jnp.float32
BF16 = jnp.bfloat16
COL_PARTS = 2
TILE = 256
CHUNKS = (((0, 0), (1, 0)), ((0, 1), (1, 1), (2, 0), (3, 0)), ((2, 1), (3, 1)))
SUMS = ("two", "tri", "two",)
GATHERS = ("two", "two", "two",)
PLAN = (
    "h0", "b00", "b10", "t0", "b01", "m0", "r0", "b20", "b11", "a0", "b30", "t1", "g0",
    "e0", "b21", "b31", "t2", "m1", "r1", "a1", "p0", "m2", "r2", "x0", "a2", "u0", "e1",
    "g1", "e2", "g2", "l0", "x1", "l1", "l2",
)
ANYWHERE = pl.BlockSpec(memory_space=pl.ANY)
TOKEN = jax.ShapeDtypeStruct((8, 128), F32)
COSTS = {
    "h0": 40000000000, "t0": 10000000000, "a0": 6000000000, "t1": 40000000000,
    "t2": 6000000000, "a1": 10000000000, "p0": 35100000000, "a2": 6000000000,
    "l0": 4199999999, "l1": 1000, "l2": 80000000000,
}


def from_behind(block, axis, distance):
    devices = range(lax.axis_size(axis))
    route = [((i - distance) % len(devices), i) for i in devices]
    return lax.ppermute(block, axis, route)


def normal_cdf(inputs):
    return 0.5 * (1.0 + jax.scipy.special.erf(inputs * (1.0 / math.sqrt(2.0))))


def gelu_value(inputs):
    return inputs * normal_cdf(inputs)


def gelu_slope(inputs):
    return normal_cdf(inputs) + inputs * jnp.exp(-0.5 * inputs * inputs) * (
        1.0 / math.sqrt(2.0 * math.pi)
    )


def hidden_of(hidden_pre):
    return gelu_value(hidden_pre.astype(F32)).astype(BF16)


def act_grad_of(incoming, down, hidden_pre):
    back = lax.dot_general(incoming, down, (((1,), (1,)), ((), ())), preferred_element_type=F32)
    scale = 1.0 / math.sqrt(down.shape[1])
    return (back * scale * gelu_slope(hidden_pre.astype(F32))).astype(BF16)


def term_of(hidden, columns, token_total):
    product = lax.dot_general(
        hidden, columns, (((0,), (0,)), ((), ())), preferred_element_type=F32
    )
    return (product * (1.0 / math.sqrt(token_total))).astype(BF16)


def adam(gradient, moment, second, rows):
    new_m = 0.9 * moment + 0.1 * gradient
    new_v = 0.95 * second + 0.05 * gradient * gradient
    fresh = (rows.astype(F32) - 0.2 * new_m / (jnp.sqrt(new_v) + 1e-08)).astype(BF16)
    return new_m, new_v, fresh


def plain(handoff, hidden_pre, down_weight, up_weight, moment, second):
    arrived = from_behind(handoff, "pipe", -1)
    incoming = lax.all_gather(arrived, "tensor", axis=2, tiled=True)[0]
    model_width = incoming.shape[1]
    shard_rows = moment.shape[1]
    hidden_total = down_weight.shape[1] * lax.axis_size("tensor")
    token_total = incoming.shape[0] * lax.axis_size("dp")
    hidden = hidden_of(hidden_pre[0])
    act_grad = act_grad_of(incoming, down_weight[0], hidden_pre[0])
    partial_value = jnp.dot(act_grad, up_weight[0], preferred_element_type=F32) * (
        1.0 / math.sqrt(hidden_total)
    )
    input_grad = lax.psum_scatter(
        partial_value.astype(BF16), "tensor", scatter_dimension=1, tiled=True
    )
    gradient = lax.psum_scatter(
        term_of(hidden, incoming, token_total), "dp", scatter_dimension=0, tiled=True
    ).astype(F32)
    own_rows = lax.dynamic_slice_in_dim(
        down_weight[0], lax.axis_index("dp") * shard_rows, shard_rows, 0
    )
    new_m, new_v, fresh = adam(gradient, moment[0], second[0], own_rows)
    new_down = lax.all_gather(fresh, "dp", axis=0, tiled=True)
    return (input_grad[None], new_down[None], new_m[None], new_v[None])


def cost(item):
    return pl.CostEstimate(flops=COSTS[item], bytes_accessed=1024, transcendentals=0)


def params(mib):
    return pltpu.CompilerParams(vmem_limit_bytes=mib * 2**20)


def prepare(hidden_pre, model_width, after, item):
    tokens, units = hidden_pre.shape
    scale = 1.0 / math.sqrt(model_width)

    def kernel(pre_ref, *refs):
        hidden_ref, slope_ref, token_ref = refs[len(after) :]
        token_ref[...] = jnp.zeros_like(token_ref)
        pre = pre_ref[...].astype(F32)
        phi = 0.5 * (1.0 + lax.erf(pre * (1.0 / math.sqrt(2.0))))
        hidden_ref[...] = (pre * phi).astype(BF16).T
        bell = jnp.exp(-0.5 * pre * pre) * (1.0 / math.sqrt(2.0 * math.pi))
        slope_ref[...] = ((phi + pre * bell) * scale).astype(BF16)

    return pl.pallas_call(
        kernel,
        grid=(tokens // TILE,),
        in_specs=[pl.BlockSpec((TILE, units), lambda i: (i, 0))] + [ANYWHERE] * len(after),
        out_specs=[
            pl.BlockSpec((units, TILE), lambda i: (0, i)),
            pl.BlockSpec((TILE, units), lambda i: (i, 0)),
            pl.BlockSpec((8, 128), lambda i: (0, 0)),
        ],
        out_shape=[
            jax.ShapeDtypeStruct((units, tokens), BF16),
            jax.ShapeDtypeStruct((tokens, units), BF16),
            TOKEN,
        ],
        compiler_params=params(8),
        cost_estimate=cost(item),
        name="prepare",
    )(hidden_pre, *after)


def terms(hidden_t, pieces, places, scale, paired, after, item):
    units, tokens = hidden_t.shape
    size, width = units // 4, pieces[0].shape[1]
    count, wide = len(pieces), len(pieces) * pieces[0].shape[1]
    heights = [size, size, 2 * size] if paired else [size] * 4
    number = len(heights)

    def kernel(places_ref, hidden_ref, *refs):
        piece_refs, refs = refs[:count], refs[count + len(after) :]
        out_refs, token_ref, joined = refs[:number], refs[number], refs[number + 1]
        step = pl.program_id(0)

        @pl.when(step == 0)
        def _():
            token_ref[...] = jnp.zeros_like(token_ref)
            for j in range(count):
                joined[:, j * width : (j + 1) * width] = piece_refs[j][...]

        product = jnp.dot(hidden_ref[...], joined[...], preferred_element_type=F32)
        product = (product * scale).astype(BF16)
        for j in range(4):
            @pl.when(step == j)
            def _(j=j):
                if paired and j >= 2:
                    out_refs[2][(j - 2) * size : (j - 1) * size, :] = product
                else:
                    out_refs[j][...] = product

    return pl.pallas_call(
        kernel,
        grid_spec=pltpu.PrefetchScalarGridSpec(
            num_scalar_prefetch=1,
            grid=(4,),
            in_specs=[pl.BlockSpec((size, tokens), lambda i, places: (places[i], 0))]
            + [pl.BlockSpec((tokens, width), lambda i, places: (0, 0))] * count
            + [ANYWHERE] * len(after),
            out_specs=[pl.BlockSpec((height, wide), lambda i, places: (0, 0)) for height in heights]
            + [pl.BlockSpec((8, 128), lambda i, places: (0, 0))],
            scratch_shapes=[pltpu.VMEM((tokens, wide), BF16)],
        ),
        out_shape=[jax.ShapeDtypeStruct((height, wide), BF16) for height in heights] + [TOKEN],
        compiler_params=params(16),
        cost_estimate=cost(item),
        name="terms",
    )(places, hidden_t, *pieces, *after)


def adam_chunk(shares, near, moment, second, down, columns, rank, previous, width, after, item):
    size, wide = shares[0].shape
    count = wide // width
    total = moment.shape[1]
    number = len(shares) + len(near)

    def kernel(columns_ref, rank_ref, *refs):
        m_ref, v_ref, down_ref = refs[number : number + 3]
        fresh_ref, new_m_ref, new_v_ref, token_ref = refs[-4:]
        token_ref[...] = jnp.zeros_like(token_ref)
        gradient = refs[0][...].astype(F32)
        for ref in refs[1:number]:
            gradient += ref[...].astype(F32)
        new_m = 0.9 * m_ref[...] + 0.1 * gradient
        new_v = 0.95 * v_ref[...] + 0.05 * gradient * gradient
        new_m_ref[...] = new_m
        new_v_ref[...] = new_v
        rows = down_ref[...].astype(F32)
        fresh_ref[...] = (rows - 0.2 * new_m / (jnp.sqrt(new_v) + 1e-08)).astype(BF16)

    here = pl.BlockSpec((size, width), lambda j, columns, rank: (0, j))
    below = pl.BlockSpec((size, width), lambda j, columns, rank: (1, j))
    there = pl.BlockSpec((size, width), lambda j, columns, rank: (0, columns[j]))
    return pl.pallas_call(
        kernel,
        grid_spec=pltpu.PrefetchScalarGridSpec(
            num_scalar_prefetch=2,
            grid=(count,),
            in_specs=[here] * len(shares)
            + [below] * len(near)
            + [there] * 2
            + [pl.BlockSpec((size, width), lambda j, columns, rank: (rank[0], columns[j]))]
            + [ANYWHERE] * (len(after) + len(previous)),
            out_specs=[here, there, there, pl.BlockSpec((8, 128), lambda j, columns, rank: (0, 0))],
        ),
        out_shape=[
            jax.ShapeDtypeStruct((size, wide), BF16),
            jax.ShapeDtypeStruct((size, total), F32),
            jax.ShapeDtypeStruct((size, total), F32),
            TOKEN,
        ],
        input_output_aliases={
            number + len(after) + 5: 1, number + len(after) + 6: 2
        } if previous else {},
        compiler_params=params(8),
        cost_estimate=cost(item),
        name="adam",
    )(columns, rank, *shares, *near, moment, second, down, *after, *previous)


def place_rows(shards, rows, columns, previous, total, width, after, item):
    size, wide = shards[0].shape
    count = wide // width
    number = len(shards)

    def kernel(rows_ref, columns_ref, *refs):
        shard_refs, out_ref, token_ref, sems = refs[:number], refs[-3], refs[-2], refs[-1]
        token_ref[...] = jnp.zeros_like(token_ref)
        copies = []
        for k in range(number):
            for j in range(count):
                copies.append(
                    pltpu.make_async_copy(
                        shard_refs[k].at[:, pl.ds(j * width, width)],
                        out_ref.at[
                            pl.ds(pl.multiple_of(rows_ref[k] * size, size), size),
                            pl.ds(pl.multiple_of(columns_ref[j] * width, width), width),
                        ],
                        sems.at[k, j],
                    )
                )
        for copy in copies:
            copy.start()
        for copy in copies:
            copy.wait()

    return pl.pallas_call(
        kernel,
        grid_spec=pltpu.PrefetchScalarGridSpec(
            num_scalar_prefetch=2,
            grid=(1,),
            in_specs=[ANYWHERE] * (number + len(after) + len(previous)),
            out_specs=[ANYWHERE, pl.BlockSpec((8, 128), lambda i, rows, columns: (0, 0))],
            scratch_shapes=[pltpu.SemaphoreType.DMA((number, count))],
        ),
        out_shape=[jax.ShapeDtypeStruct(total, BF16), TOKEN],
        input_output_aliases={2 + number + len(after): 0} if previous else {},
        compiler_params=params(8),
        cost_estimate=cost(item),
        name="place",
    )(rows, columns, *shards, *after, *previous)


def partials(pieces, where, order, slope, down, up, scale, after, item):
    tokens, units = slope.shape
    model_width = down.shape[1]
    width = pieces[0].shape[1]
    count = len(pieces)
    block = model_width // 4
    rows = tokens
    step = 2 * TILE

    def kernel(where_ref, order_ref, *refs):
        piece_refs, refs = refs[:count], refs[count:]
        slope_ref, down_ref, up_ref = refs[:3]
        outs, token_ref, joined, product_ref = refs[3 + len(after) : -3], *refs[-3:]
        token_ref[...] = jnp.zeros_like(token_ref)
        for j in range(count):
            joined[:, pl.ds(pl.multiple_of(where_ref[j] * width, width), width)] = piece_refs[j][...]
        back = lax.dot_general(
            joined[...], down_ref[...], (((1,), (1,)), ((), ())), preferred_element_type=F32
        )
        act_grad = (back * slope_ref[...].astype(F32)).astype(BF16)
        product = jnp.dot(act_grad, up_ref[...], preferred_element_type=F32) * scale
        product_ref[...] = product.astype(BF16)

        for k in range(4):
            first = pl.multiple_of(order_ref[k] * block, block)
            outs[k][...] = product_ref[:, pl.ds(first, block)]

    return pl.pallas_call(
        kernel,
        grid_spec=pltpu.PrefetchScalarGridSpec(
            num_scalar_prefetch=2,
            grid=(rows // step,),
            in_specs=[pl.BlockSpec((step, width), lambda i, w, o: (i, 0))] * count
            + [pl.BlockSpec((step, units), lambda i, w, o: (i, 0))]
            + [pl.BlockSpec((units, model_width), lambda i, w, o: (0, 0))] * 2
            + [ANYWHERE] * len(after),
            out_specs=[
                pl.BlockSpec((step, block), lambda i, w, o: (i, 0)),
            ]
            * 4
            + [pl.BlockSpec((8, 128), lambda i, w, o: (0, 0))],
            scratch_shapes=[
                pltpu.VMEM((step, model_width), BF16),
                pltpu.VMEM((step, model_width), BF16),
            ],
        ),
        out_shape=[
            jax.ShapeDtypeStruct((rows, block), BF16),
        ]
        * 4
        + [TOKEN],
        compiler_params=params(28),
        cost_estimate=cost(item),
        name="partials",
    )(where, order, *pieces, slope, down, up, *after)


def on_device(handoff, hidden_pre, down_weight, up_weight, moment, second):
    rank = lax.axis_index("dp")
    tensor = lax.axis_index("tensor")
    handoff, hidden_pre, down, up = handoff[0], hidden_pre[0], down_weight[0], up_weight[0]
    tokens, block = handoff.shape
    width = block // COL_PARTS
    model_width = down.shape[1]

    def swapped(value, axis, distance):
        return lax.ppermute(value, axis, [(i, i ^ distance) for i in range(4)])

    def column_of(key):
        return (tensor ^ key[0]) * COL_PARTS + key[1]

    def columns_of(keys):
        return jnp.stack([column_of(key) for key in keys]).astype(jnp.int32)

    shards = jnp.stack([rank, rank ^ 1, rank ^ 2, rank ^ 3]).astype(jnp.int32)
    paired = jnp.stack([rank, rank ^ 2, rank ^ 3, rank ^ 1]).astype(jnp.int32)
    rank_now = rank.astype(jnp.int32)[None]
    order = jnp.stack([tensor, tensor ^ 2, tensor ^ 1, tensor ^ 3]).astype(jnp.int32)
    term_scale = 1.0 / math.sqrt(tokens * 4)
    partial_scale = 1.0 / math.sqrt(down.shape[0] * 4)
    columns = [columns_of(chunk) for chunk in CHUNKS]
    keys = [(b, g) for g in range(COL_PARTS) for b in range(4)]
    where = columns_of(keys)
    held, values, moments, new_down = [], {}, [], []

    def after():
        out = list(held)
        held.clear()
        return out

    def arrive(name):
        values[name], *held[:] = lax.optimization_barrier((values[name], values["token"], *held))
        held.append(values[name])

    for part in range(COL_PARTS):
        columns_now = handoff[:, part * width : (part + 1) * width]
        values["b0" + str(part)] = from_behind(columns_now, "pipe", -1)

    for name in PLAN:
        kind, k = name[0], int(name[1])
        if kind == "h":
            values["hidden"], values["slope"], values["token"] = prepare(
                hidden_pre, model_width, [shards, paired, rank_now, order, where, *columns],
                name,
            )
        elif kind == "b":
            arrive(name)
            part = name[2]
            if k == 0:
                values["b1" + part] = swapped(values[name], "tensor", 1)
                values["b2" + part] = swapped(values[name], "tensor", 2)
            elif k == 2:
                values["b3" + part] = swapped(values[name], "tensor", 1)
        elif kind == "t":
            pieces = [values["b%d%d" % key] for key in CHUNKS[k]]
            pair, step = SUMS[k] == "two", SUMS[k] == "tri"
            *out, values["token"] = terms(
                values["hidden"], pieces, paired if pair else shards, term_scale, pair, after(), name
            )
            if pair:
                values["s0" + name[1]], values["s2" + name[1]] = out[:2]
                values["m" + name[1]] = swapped(out[2], "dp", 1)
            else:
                values["s0" + name[1]], values["s2" + name[1]] = out[0], out[2]
                values["m" + name[1]] = swapped(out[3], "dp", 1) if step else None
                for j in (1,) if step else (3, 2, 1):
                    values["s%d%d" % (j, k)] = swapped(out[j], "dp", j)
        elif kind == "m":
            arrive(name)
            size = values["s0" + name[1]].shape[0]
            held_part = values[name][:size] if SUMS[k] == "two" else values[name]
            far = values["s2" + name[1]].astype(F32) + held_part.astype(F32)
            values["s2" + name[1]] = swapped(far.astype(BF16), "dp", 2)
        elif kind == "r":
            for j in {"two": (2,), "tri": (1, 2), "one": (3, 2, 1)}[SUMS[k]]:
                arrive("s%d%d" % (j, k))
        elif kind == "a":
            if SUMS[k] == "two":
                shares, near = [values["s%d%d" % (j, k)] for j in (0, 2)], [values["m" + name[1]]]
            else:
                number = 3 if SUMS[k] == "tri" else 4
                shares, near = [values["s%d%d" % (j, k)] for j in range(number)], []
            fresh, *moments[:], values["token"] = adam_chunk(
                shares, near, moment[0], second[0], down, columns[k], rank_now,
                moments, width, after(), name,
            )
            values["g0" + name[1]] = fresh
            values["g2" + name[1]] = swapped(fresh, "dp", 2)
            values["g1" + name[1]] = swapped(fresh, "dp", 1)
            if GATHERS[k] == "one":
                values["g3" + name[1]] = swapped(fresh, "dp", 3)
        elif kind == "g":
            arrive("g2" + name[1])
            if GATHERS[k] != "one":
                values["g3" + name[1]] = swapped(values["g2" + name[1]], "dp", 1)
        elif kind == "e":
            arrive("g1" + name[1])
        elif kind == "l":
            gathered = [values["g%d%d" % (j, k)] for j in range(4)]
            *new_down[:], values["token"] = place_rows(
                gathered, shards, columns[k], new_down, down.shape, width, after(), name
            )
        elif kind == "p":
            pieces = [values["b%d%d" % key] for key in keys]
            values["own"], values["other"], values["x2"], values["x0"], values["token"] = partials(
                pieces, where, order, values["slope"], down, up, partial_scale, after(), name
            )
            values["x2"] = swapped(values["x2"], "tensor", 1)
            if "w0" not in PLAN:
                values["x0"] = swapped(values["x0"], "tensor", 1)
        elif kind == "w":
            arrive("x0")
            values["x0"] = swapped(values["x0"], "tensor", 1)
        elif kind == "u":
            arrive("x2")
        elif kind == "x" and k == 0:
            arrive("x0")
            other = values["other"].astype(F32) + values["x0"].astype(F32)
            values["x1"] = swapped(other.astype(BF16), "tensor", 2)
        elif kind == "x":
            arrive("x1")
            own = values["own"].astype(F32) + values["x2"].astype(F32)
            input_grad = (own + values["x1"].astype(F32)).astype(BF16)
    return (input_grad[None], new_down[0][None], moments[0][None], moments[1][None])


def solution(mesh):
    placed = (
        P("pipe", "dp", "tensor"),
        P("pipe", "dp", "tensor"),
        P("pipe", "tensor", None),
        P("pipe", "tensor", None),
        P("pipe", ("tensor", "dp"), None),
        P("pipe", ("tensor", "dp"), None),
    )
    fits = mesh.shape["tensor"] == 4 and mesh.shape["dp"] == 4
    return jax.shard_map(
        on_device if fits else plain,
        mesh=mesh,
        in_specs=placed,
        out_specs=(
            P("pipe", "dp", "tensor"),
            P("pipe", "tensor", None),
            P("pipe", ("tensor", "dp"), None),
            P("pipe", ("tensor", "dp"), None),
        ),
        check_vma=False,
    )
```

```python
import math

import jax
import jax.numpy as jnp
from jax import lax
from jax.experimental import pallas as pl
from jax.experimental.pallas import tpu as pltpu
from jax.sharding import PartitionSpec as P

F32 = jnp.float32
BF16 = jnp.bfloat16
COL_PARTS = 2
TILE = 256
CHUNKS = (((0, 0), (1, 0)), ((0, 1), (1, 1), (2, 0), (3, 0)), ((2, 1), (3, 1)))
SUMS = ("two", "tri", "two",)
GATHERS = ("two", "two", "two",)
PLAN = (
    "h0", "b00", "b10", "t0", "b01", "m0", "b20", "b11", "r0", "a0", "b30", "t1", "g0",
    "e0", "b21", "b31", "t2", "m1", "r1", "a1", "p0", "m2", "r2", "x0", "a2", "u0", "e1",
    "g1", "e2", "g2", "l0", "x1", "l1", "l2",
)
ANYWHERE = pl.BlockSpec(memory_space=pl.ANY)
INSIDE = pl.BlockSpec(memory_space=pltpu.VMEM)
TOKEN = jax.ShapeDtypeStruct((8, 128), F32)
COSTS = {
    "h0": 40000000000, "t0": 10000000000, "a0": 10000000000, "t1": 40000000000,
    "t2": 6000000000, "a1": 10000000000, "p0": 3000000000, "a2": 6000000000, "l0": 4199999999,
    "l1": 1000, "l2": 80000000000,
}


def from_behind(block, axis, distance):
    devices = range(lax.axis_size(axis))
    route = [((i - distance) % len(devices), i) for i in devices]
    return lax.ppermute(block, axis, route)


def normal_cdf(inputs):
    return 0.5 * (1.0 + jax.scipy.special.erf(inputs * (1.0 / math.sqrt(2.0))))


def gelu_value(inputs):
    return inputs * normal_cdf(inputs)


def gelu_slope(inputs):
    return normal_cdf(inputs) + inputs * jnp.exp(-0.5 * inputs * inputs) * (
        1.0 / math.sqrt(2.0 * math.pi)
    )


def hidden_of(hidden_pre):
    return gelu_value(hidden_pre.astype(F32)).astype(BF16)


def act_grad_of(incoming, down, hidden_pre):
    back = lax.dot_general(incoming, down, (((1,), (1,)), ((), ())), preferred_element_type=F32)
    scale = 1.0 / math.sqrt(down.shape[1])
    return (back * scale * gelu_slope(hidden_pre.astype(F32))).astype(BF16)


def term_of(hidden, columns, token_total):
    product = lax.dot_general(
        hidden, columns, (((0,), (0,)), ((), ())), preferred_element_type=F32
    )
    return (product * (1.0 / math.sqrt(token_total))).astype(BF16)


def adam(gradient, moment, second, rows):
    new_m = 0.9 * moment + 0.1 * gradient
    new_v = 0.95 * second + 0.05 * gradient * gradient
    fresh = (rows.astype(F32) - 0.2 * new_m / (jnp.sqrt(new_v) + 1e-08)).astype(BF16)
    return new_m, new_v, fresh


def plain(handoff, hidden_pre, down_weight, up_weight, moment, second):
    arrived = from_behind(handoff, "pipe", -1)
    incoming = lax.all_gather(arrived, "tensor", axis=2, tiled=True)[0]
    model_width = incoming.shape[1]
    shard_rows = moment.shape[1]
    hidden_total = down_weight.shape[1] * lax.axis_size("tensor")
    token_total = incoming.shape[0] * lax.axis_size("dp")
    hidden = hidden_of(hidden_pre[0])
    act_grad = act_grad_of(incoming, down_weight[0], hidden_pre[0])
    partial_value = jnp.dot(act_grad, up_weight[0], preferred_element_type=F32) * (
        1.0 / math.sqrt(hidden_total)
    )
    input_grad = lax.psum_scatter(
        partial_value.astype(BF16), "tensor", scatter_dimension=1, tiled=True
    )
    gradient = lax.psum_scatter(
        term_of(hidden, incoming, token_total), "dp", scatter_dimension=0, tiled=True
    ).astype(F32)
    own_rows = lax.dynamic_slice_in_dim(
        down_weight[0], lax.axis_index("dp") * shard_rows, shard_rows, 0
    )
    new_m, new_v, fresh = adam(gradient, moment[0], second[0], own_rows)
    new_down = lax.all_gather(fresh, "dp", axis=0, tiled=True)
    return (input_grad[None], new_down[None], new_m[None], new_v[None])


def cost(item):
    return pl.CostEstimate(flops=COSTS[item], bytes_accessed=1024, transcendentals=0)


def params(mib):
    return pltpu.CompilerParams(vmem_limit_bytes=mib * 2**20)


def prepare(hidden_pre, model_width, after, item):
    tokens, units = hidden_pre.shape
    scale = 1.0 / math.sqrt(model_width)

    def kernel(pre_ref, *refs):
        hidden_ref, slope_ref, token_ref = refs[len(after) :]
        token_ref[...] = jnp.zeros_like(token_ref)
        pre = pre_ref[...].astype(F32)
        phi = 0.5 * (1.0 + lax.erf(pre * (1.0 / math.sqrt(2.0))))
        hidden_ref[...] = (pre * phi).astype(BF16).T
        bell = jnp.exp(-0.5 * pre * pre) * (1.0 / math.sqrt(2.0 * math.pi))
        slope_ref[...] = ((phi + pre * bell) * scale).astype(BF16)

    return pl.pallas_call(
        kernel,
        grid=(tokens // TILE,),
        in_specs=[pl.BlockSpec((TILE, units), lambda i: (i, 0))] + [ANYWHERE] * len(after),
        out_specs=[
            pl.BlockSpec((units, TILE), lambda i: (0, i)),
            pl.BlockSpec((TILE, units), lambda i: (i, 0)),
            pl.BlockSpec((8, 128), lambda i: (0, 0)),
        ],
        out_shape=[
            jax.ShapeDtypeStruct((units, tokens), BF16),
            jax.ShapeDtypeStruct((tokens, units), BF16),
            TOKEN,
        ],
        compiler_params=params(8),
        cost_estimate=cost(item),
        name="prepare",
    )(hidden_pre, *after)


def terms(hidden_t, pieces, places, scale, paired, after, item):
    units, tokens = hidden_t.shape
    size, width = units // 4, pieces[0].shape[1]
    count, wide = len(pieces), len(pieces) * pieces[0].shape[1]
    heights = [size, size, 2 * size] if paired else [size] * 4
    number = len(heights)

    def kernel(places_ref, hidden_ref, *refs):
        piece_refs, refs = refs[:count], refs[count + len(after) :]
        out_refs, token_ref, joined, product = refs[:number], *refs[number:]
        token_ref[...] = jnp.zeros_like(token_ref)
        for j in range(count):
            joined[:, j * width : (j + 1) * width] = piece_refs[j][...]
        whole = jnp.dot(hidden_ref[...], joined[...], preferred_element_type=F32)
        product[...] = (whole * scale).astype(BF16)
        for j in range(4):
            rows = product[pl.ds(pl.multiple_of(places_ref[j] * size, size), size), :]
            if paired and j >= 2:
                out_refs[2][(j - 2) * size : (j - 1) * size, :] = rows
            else:
                out_refs[j][...] = rows

    return pl.pallas_call(
        kernel,
        in_specs=[pl.BlockSpec(memory_space=pltpu.SMEM)]
        + [INSIDE] * (1 + count)
        + [ANYWHERE] * len(after),
        out_specs=[INSIDE] * (number + 1),
        scratch_shapes=[pltpu.VMEM((tokens, wide), BF16), pltpu.VMEM((units, wide), BF16)],
        out_shape=[jax.ShapeDtypeStruct((height, wide), BF16) for height in heights] + [TOKEN],
        compiler_params=params(16),
        cost_estimate=cost(item),
        name="terms",
    )(places, hidden_t, *pieces, *after)


def adam_chunk(shares, near, moment, second, down, columns, rank, previous, width, after, item):
    size, wide = shares[0].shape
    count = wide // width
    total = moment.shape[1]
    number = len(shares) + len(near)

    def kernel(columns_ref, rank_ref, *refs):
        m_ref, v_ref, down_ref = refs[number : number + 3]
        fresh_ref, new_m_ref, new_v_ref, token_ref = refs[-4:]
        token_ref[...] = jnp.zeros_like(token_ref)
        gradient = refs[0][...].astype(F32)
        for ref in refs[1:number]:
            gradient += ref[...].astype(F32)
        new_m = 0.9 * m_ref[...] + 0.1 * gradient
        new_v = 0.95 * v_ref[...] + 0.05 * gradient * gradient
        new_m_ref[...] = new_m
        new_v_ref[...] = new_v
        rows = down_ref[...].astype(F32)
        fresh_ref[...] = (rows - 0.2 * new_m / (jnp.sqrt(new_v) + 1e-08)).astype(BF16)

    here = pl.BlockSpec((size, width), lambda j, columns, rank: (0, j))
    below = pl.BlockSpec((size, width), lambda j, columns, rank: (1, j))
    there = pl.BlockSpec((size, width), lambda j, columns, rank: (0, columns[j]))
    return pl.pallas_call(
        kernel,
        grid_spec=pltpu.PrefetchScalarGridSpec(
            num_scalar_prefetch=2,
            grid=(count,),
            in_specs=[here] * len(shares)
            + [below] * len(near)
            + [there] * 2
            + [pl.BlockSpec((size, width), lambda j, columns, rank: (rank[0], columns[j]))]
            + [ANYWHERE] * (len(after) + len(previous)),
            out_specs=[here, there, there, pl.BlockSpec((8, 128), lambda j, columns, rank: (0, 0))],
        ),
        out_shape=[
            jax.ShapeDtypeStruct((size, wide), BF16),
            jax.ShapeDtypeStruct((size, total), F32),
            jax.ShapeDtypeStruct((size, total), F32),
            TOKEN,
        ],
        input_output_aliases={
            number + len(after) + 5: 1, number + len(after) + 6: 2
        } if previous else {},
        compiler_params=params(8),
        cost_estimate=cost(item),
        name="adam",
    )(columns, rank, *shares, *near, moment, second, down, *after, *previous)


def place_rows(shards, rows, columns, previous, total, width, after, item):
    size, wide = shards[0].shape
    count = wide // width
    number = len(shards)

    def kernel(rows_ref, columns_ref, *refs):
        shard_refs, out_ref, token_ref, sems = refs[:number], refs[-3], refs[-2], refs[-1]
        token_ref[...] = jnp.zeros_like(token_ref)
        copies = []
        for k in range(number):
            for j in range(count):
                copies.append(
                    pltpu.make_async_copy(
                        shard_refs[k].at[:, pl.ds(j * width, width)],
                        out_ref.at[
                            pl.ds(pl.multiple_of(rows_ref[k] * size, size), size),
                            pl.ds(pl.multiple_of(columns_ref[j] * width, width), width),
                        ],
                        sems.at[k, j],
                    )
                )
        for copy in copies:
            copy.start()
        for copy in copies:
            copy.wait()

    return pl.pallas_call(
        kernel,
        grid_spec=pltpu.PrefetchScalarGridSpec(
            num_scalar_prefetch=2,
            grid=(1,),
            in_specs=[ANYWHERE] * (number + len(after) + len(previous)),
            out_specs=[ANYWHERE, pl.BlockSpec((8, 128), lambda i, rows, columns: (0, 0))],
            scratch_shapes=[pltpu.SemaphoreType.DMA((number, count))],
        ),
        out_shape=[jax.ShapeDtypeStruct(total, BF16), TOKEN],
        input_output_aliases={2 + number + len(after): 0} if previous else {},
        compiler_params=params(8),
        cost_estimate=cost(item),
        name="place",
    )(rows, columns, *shards, *after, *previous)


def partials(pieces, where, order, slope, down, up, scale, after, item):
    tokens, units = slope.shape
    model_width = down.shape[1]
    width = pieces[0].shape[1]
    count = len(pieces)
    block = model_width // 4
    rows = tokens
    step = 2 * TILE

    def kernel(where_ref, order_ref, *refs):
        piece_refs, refs = refs[:count], refs[count:]
        slope_ref, down_ref, up_ref = refs[:3]
        outs, token_ref, joined, product_ref = refs[3 + len(after) : -3], *refs[-3:]
        token_ref[...] = jnp.zeros_like(token_ref)
        for j in range(count):
            joined[:, pl.ds(pl.multiple_of(where_ref[j] * width, width), width)] = piece_refs[j][...]
        back = lax.dot_general(
            joined[...], down_ref[...], (((1,), (1,)), ((), ())), preferred_element_type=F32
        )
        act_grad = (back * slope_ref[...].astype(F32)).astype(BF16)
        product = jnp.dot(act_grad, up_ref[...], preferred_element_type=F32) * scale
        product_ref[...] = product.astype(BF16)

        for k in range(4):
            first = pl.multiple_of(order_ref[k] * block, block)
            outs[k][...] = product_ref[:, pl.ds(first, block)]

    return pl.pallas_call(
        kernel,
        grid_spec=pltpu.PrefetchScalarGridSpec(
            num_scalar_prefetch=2,
            grid=(rows // step,),
            in_specs=[pl.BlockSpec((step, width), lambda i, w, o: (i, 0))] * count
            + [pl.BlockSpec((step, units), lambda i, w, o: (i, 0))]
            + [pl.BlockSpec((units, model_width), lambda i, w, o: (0, 0))] * 2
            + [ANYWHERE] * len(after),
            out_specs=[
                pl.BlockSpec((step, block), lambda i, w, o: (i, 0)),
            ]
            * 4
            + [pl.BlockSpec((8, 128), lambda i, w, o: (0, 0))],
            scratch_shapes=[
                pltpu.VMEM((step, model_width), BF16),
                pltpu.VMEM((step, model_width), BF16),
            ],
        ),
        out_shape=[
            jax.ShapeDtypeStruct((rows, block), BF16),
        ]
        * 4
        + [TOKEN],
        compiler_params=params(28),
        cost_estimate=cost(item),
        name="partials",
    )(where, order, *pieces, slope, down, up, *after)


def on_device(handoff, hidden_pre, down_weight, up_weight, moment, second):
    rank = lax.axis_index("dp")
    tensor = lax.axis_index("tensor")
    handoff, hidden_pre, down, up = handoff[0], hidden_pre[0], down_weight[0], up_weight[0]
    tokens, block = handoff.shape
    width = block // COL_PARTS
    model_width = down.shape[1]

    def swapped(value, axis, distance):
        return lax.ppermute(value, axis, [(i, i ^ distance) for i in range(4)])

    def column_of(key):
        return (tensor ^ key[0]) * COL_PARTS + key[1]

    def columns_of(keys):
        return jnp.stack([column_of(key) for key in keys]).astype(jnp.int32)

    shards = jnp.stack([rank, rank ^ 1, rank ^ 2, rank ^ 3]).astype(jnp.int32)
    paired = jnp.stack([rank, rank ^ 2, rank ^ 3, rank ^ 1]).astype(jnp.int32)
    rank_now = rank.astype(jnp.int32)[None]
    order = jnp.stack([tensor, tensor ^ 2, tensor ^ 1, tensor ^ 3]).astype(jnp.int32)
    term_scale = 1.0 / math.sqrt(tokens * 4)
    partial_scale = 1.0 / math.sqrt(down.shape[0] * 4)
    columns = [columns_of(chunk) for chunk in CHUNKS]
    keys = [(b, g) for g in range(COL_PARTS) for b in range(4)]
    where = columns_of(keys)
    held, values, moments, new_down = [], {}, [], []

    def after():
        out = list(held)
        held.clear()
        return out

    def arrive(name):
        values[name], *held[:] = lax.optimization_barrier((values[name], values["token"], *held))
        held.append(values[name])

    for part in range(COL_PARTS):
        columns_now = handoff[:, part * width : (part + 1) * width]
        values["b0" + str(part)] = from_behind(columns_now, "pipe", -1)

    for name in PLAN:
        kind, k = name[0], int(name[1])
        if kind == "h":
            values["hidden"], values["slope"], values["token"] = prepare(
                hidden_pre, model_width, [shards, paired, rank_now, order, where, *columns],
                name,
            )
        elif kind == "b":
            arrive(name)
            part = name[2]
            if k == 0:
                values["b1" + part] = swapped(values[name], "tensor", 1)
                values["b2" + part] = swapped(values[name], "tensor", 2)
            elif k == 2:
                values["b3" + part] = swapped(values[name], "tensor", 1)
        elif kind == "t":
            pieces = [values["b%d%d" % key] for key in CHUNKS[k]]
            pair, step = SUMS[k] == "two", SUMS[k] in ("tri", "trd")
            *out, values["token"] = terms(
                values["hidden"], pieces, paired if pair else shards, term_scale, pair, after(), name
            )
            if pair:
                values["s0" + name[1]], values["s2" + name[1]] = out[:2]
                values["m" + name[1]] = swapped(out[2], "dp", 1)
            else:
                values["s0" + name[1]], values["s2" + name[1]] = out[0], out[2]
                values["m" + name[1]] = swapped(out[3], "dp", 1) if step else None
                values["s1" + name[1]] = out[1]
                for j in {"tri": (1,), "trd": (), "one": (3, 2, 1)}[SUMS[k]]:
                    values["s%d%d" % (j, k)] = swapped(out[j], "dp", j)
        elif kind == "m":
            arrive(name)
            size = values["s0" + name[1]].shape[0]
            held_part = values[name][:size] if SUMS[k] == "two" else values[name]
            far = values["s2" + name[1]].astype(F32) + held_part.astype(F32)
            far = far.astype(BF16)
            if SUMS[k] == "trd":
                far, near = lax.optimization_barrier((far, values["s1" + name[1]]))
                values["s1" + name[1]] = swapped(near, "dp", 1)
            values["s2" + name[1]] = swapped(far, "dp", 2)
        elif kind == "r":
            for j in {"two": (2,), "tri": (1, 2), "trd": (2, 1), "one": (3, 2, 1)}[SUMS[k]]:
                arrive("s%d%d" % (j, k))
        elif kind == "a":
            if SUMS[k] == "two":
                shares, near = [values["s%d%d" % (j, k)] for j in (0, 2)], [values["m" + name[1]]]
            else:
                number = 3 if SUMS[k] in ("tri", "trd") else 4
                shares, near = [values["s%d%d" % (j, k)] for j in range(number)], []
            fresh, *moments[:], values["token"] = adam_chunk(
                shares, near, moment[0], second[0], down, columns[k], rank_now,
                moments, width, after(), name,
            )
            values["g0" + name[1]] = fresh
            values["g2" + name[1]] = swapped(fresh, "dp", 2)
            values["g1" + name[1]] = swapped(fresh, "dp", 1)
            if GATHERS[k] == "one":
                values["g3" + name[1]] = swapped(fresh, "dp", 3)
        elif kind == "g":
            arrive("g2" + name[1])
            if GATHERS[k] != "one":
                values["g3" + name[1]] = swapped(values["g2" + name[1]], "dp", 1)
        elif kind == "e":
            arrive("g1" + name[1])
        elif kind == "l":
            gathered = [values["g%d%d" % (j, k)] for j in range(4)]
            *new_down[:], values["token"] = place_rows(
                gathered, shards, columns[k], new_down, down.shape, width, after(), name
            )
        elif kind == "p":
            pieces = [values["b%d%d" % key] for key in keys]
            values["own"], values["other"], values["x2"], values["x0"], values["token"] = partials(
                pieces, where, order, values["slope"], down, up, partial_scale, after(), name
            )
            values["x2"] = swapped(values["x2"], "tensor", 1)
            if "w0" not in PLAN:
                values["x0"] = swapped(values["x0"], "tensor", 1)
        elif kind == "w":
            arrive("x0")
            values["x0"] = swapped(values["x0"], "tensor", 1)
        elif kind == "u":
            arrive("x2")
        elif kind == "x" and k == 0:
            arrive("x0")
            other = values["other"].astype(F32) + values["x0"].astype(F32)
            values["x1"] = swapped(other.astype(BF16), "tensor", 2)
        elif kind == "x":
            arrive("x1")
            own = values["own"].astype(F32) + values["x2"].astype(F32)
            input_grad = (own + values["x1"].astype(F32)).astype(BF16)
    return (input_grad[None], new_down[0][None], moments[0][None], moments[1][None])


def solution(mesh):
    placed = (
        P("pipe", "dp", "tensor"),
        P("pipe", "dp", "tensor"),
        P("pipe", "tensor", None),
        P("pipe", "tensor", None),
        P("pipe", ("tensor", "dp"), None),
        P("pipe", ("tensor", "dp"), None),
    )
    fits = mesh.shape["tensor"] == 4 and mesh.shape["dp"] == 4
    return jax.shard_map(
        on_device if fits else plain,
        mesh=mesh,
        in_specs=placed,
        out_specs=(
            P("pipe", "dp", "tensor"),
            P("pipe", "tensor", None),
            P("pipe", ("tensor", "dp"), None),
            P("pipe", ("tensor", "dp"), None),
        ),
        check_vma=False,
    )
```

```python
import math

import jax
import jax.numpy as jnp
from jax import lax
from jax.experimental import pallas as pl
from jax.experimental.pallas import tpu as pltpu
from jax.sharding import PartitionSpec as P

F32 = jnp.float32
BF16 = jnp.bfloat16
COL_PARTS = 2
TILE = 256
CHUNKS = (((0, 0), (1, 0)), ((0, 1), (1, 1), (2, 0), (3, 0)), ((2, 1), (3, 1)))
SUMS = ("two", "tri", "two",)
GATHERS = ("two", "two", "one",)
PLAN = (
    "h0", "b00", "b10", "t0", "b01", "m0", "b20", "b11", "r0", "a0", "b30", "t1", "g0",
    "e0", "b21", "b31", "t2", "m1", "r1", "a1", "p0", "m2", "r2", "x0", "a2", "u0", "g1",
    "e1", "g2", "l0", "x1", "l1", "l2",
)
ANYWHERE = pl.BlockSpec(memory_space=pl.ANY)
INSIDE = pl.BlockSpec(memory_space=pltpu.VMEM)
TOKEN = jax.ShapeDtypeStruct((8, 128), F32)
COSTS = {
    "h0": 40000000000, "t0": 10000000000, "a0": 10000000000, "t1": 40000000000,
    "t2": 6000000000, "a1": 10000000000, "p0": 3000000000, "a2": 6000000000, "l0": 4199999999,
    "l1": 1000, "l2": 6000000000,
}


def from_behind(block, axis, distance):
    devices = range(lax.axis_size(axis))
    route = [((i - distance) % len(devices), i) for i in devices]
    return lax.ppermute(block, axis, route)


def normal_cdf(inputs):
    return 0.5 * (1.0 + jax.scipy.special.erf(inputs * (1.0 / math.sqrt(2.0))))


def gelu_value(inputs):
    return inputs * normal_cdf(inputs)


def gelu_slope(inputs):
    return normal_cdf(inputs) + inputs * jnp.exp(-0.5 * inputs * inputs) * (
        1.0 / math.sqrt(2.0 * math.pi)
    )


def hidden_of(hidden_pre):
    return gelu_value(hidden_pre.astype(F32)).astype(BF16)


def act_grad_of(incoming, down, hidden_pre):
    back = lax.dot_general(incoming, down, (((1,), (1,)), ((), ())), preferred_element_type=F32)
    scale = 1.0 / math.sqrt(down.shape[1])
    return (back * scale * gelu_slope(hidden_pre.astype(F32))).astype(BF16)


def term_of(hidden, columns, token_total):
    product = lax.dot_general(
        hidden, columns, (((0,), (0,)), ((), ())), preferred_element_type=F32
    )
    return (product * (1.0 / math.sqrt(token_total))).astype(BF16)


def adam(gradient, moment, second, rows):
    new_m = 0.9 * moment + 0.1 * gradient
    new_v = 0.95 * second + 0.05 * gradient * gradient
    fresh = (rows.astype(F32) - 0.2 * new_m / (jnp.sqrt(new_v) + 1e-08)).astype(BF16)
    return new_m, new_v, fresh


def plain(handoff, hidden_pre, down_weight, up_weight, moment, second):
    arrived = from_behind(handoff, "pipe", -1)
    incoming = lax.all_gather(arrived, "tensor", axis=2, tiled=True)[0]
    model_width = incoming.shape[1]
    shard_rows = moment.shape[1]
    hidden_total = down_weight.shape[1] * lax.axis_size("tensor")
    token_total = incoming.shape[0] * lax.axis_size("dp")
    hidden = hidden_of(hidden_pre[0])
    act_grad = act_grad_of(incoming, down_weight[0], hidden_pre[0])
    partial_value = jnp.dot(act_grad, up_weight[0], preferred_element_type=F32) * (
        1.0 / math.sqrt(hidden_total)
    )
    input_grad = lax.psum_scatter(
        partial_value.astype(BF16), "tensor", scatter_dimension=1, tiled=True
    )
    gradient = lax.psum_scatter(
        term_of(hidden, incoming, token_total), "dp", scatter_dimension=0, tiled=True
    ).astype(F32)
    own_rows = lax.dynamic_slice_in_dim(
        down_weight[0], lax.axis_index("dp") * shard_rows, shard_rows, 0
    )
    new_m, new_v, fresh = adam(gradient, moment[0], second[0], own_rows)
    new_down = lax.all_gather(fresh, "dp", axis=0, tiled=True)
    return (input_grad[None], new_down[None], new_m[None], new_v[None])


def cost(item):
    return pl.CostEstimate(flops=COSTS[item], bytes_accessed=1024, transcendentals=0)


def params(mib):
    return pltpu.CompilerParams(vmem_limit_bytes=mib * 2**20)


def prepare(hidden_pre, model_width, after, item):
    tokens, units = hidden_pre.shape
    scale = 1.0 / math.sqrt(model_width)

    def kernel(pre_ref, *refs):
        hidden_ref, slope_ref, token_ref = refs[len(after) :]
        token_ref[...] = jnp.zeros_like(token_ref)
        pre = pre_ref[...].astype(F32)
        phi = 0.5 * (1.0 + lax.erf(pre * (1.0 / math.sqrt(2.0))))
        hidden_ref[...] = (pre * phi).astype(BF16).T
        bell = jnp.exp(-0.5 * pre * pre) * (1.0 / math.sqrt(2.0 * math.pi))
        slope_ref[...] = ((phi + pre * bell) * scale).astype(BF16)

    return pl.pallas_call(
        kernel,
        grid=(tokens // TILE,),
        in_specs=[pl.BlockSpec((TILE, units), lambda i: (i, 0))] + [ANYWHERE] * len(after),
        out_specs=[
            pl.BlockSpec((units, TILE), lambda i: (0, i)),
            pl.BlockSpec((TILE, units), lambda i: (i, 0)),
            pl.BlockSpec((8, 128), lambda i: (0, 0)),
        ],
        out_shape=[
            jax.ShapeDtypeStruct((units, tokens), BF16),
            jax.ShapeDtypeStruct((tokens, units), BF16),
            TOKEN,
        ],
        compiler_params=params(8),
        cost_estimate=cost(item),
        name="prepare",
    )(hidden_pre, *after)


def terms(hidden_t, pieces, places, scale, paired, after, item):
    units, tokens = hidden_t.shape
    size, width = units // 4, pieces[0].shape[1]
    count, wide = len(pieces), len(pieces) * pieces[0].shape[1]
    heights = [size, size, 2 * size] if paired else [size] * 4
    number = len(heights)

    def kernel(places_ref, hidden_ref, *refs):
        piece_refs, refs = refs[:count], refs[count + len(after) :]
        out_refs, token_ref, joined, product = refs[:number], *refs[number:]
        token_ref[...] = jnp.zeros_like(token_ref)
        for j in range(count):
            joined[:, j * width : (j + 1) * width] = piece_refs[j][...]
        whole = jnp.dot(hidden_ref[...], joined[...], preferred_element_type=F32)
        product[...] = (whole * scale).astype(BF16)
        for j in range(4):
            rows = product[pl.ds(pl.multiple_of(places_ref[j] * size, size), size), :]
            if paired and j >= 2:
                out_refs[2][(j - 2) * size : (j - 1) * size, :] = rows
            else:
                out_refs[j][...] = rows

    return pl.pallas_call(
        kernel,
        in_specs=[pl.BlockSpec(memory_space=pltpu.SMEM)]
        + [INSIDE] * (1 + count)
        + [ANYWHERE] * len(after),
        out_specs=[INSIDE] * (number + 1),
        scratch_shapes=[pltpu.VMEM((tokens, wide), BF16), pltpu.VMEM((units, wide), BF16)],
        out_shape=[jax.ShapeDtypeStruct((height, wide), BF16) for height in heights] + [TOKEN],
        compiler_params=params(16),
        cost_estimate=cost(item),
        name="terms",
    )(places, hidden_t, *pieces, *after)


def adam_chunk(shares, near, moment, second, down, columns, rank, previous, width, after, item):
    size, wide = shares[0].shape
    count = wide // width
    total = moment.shape[1]
    number = len(shares) + len(near)

    def kernel(columns_ref, rank_ref, *refs):
        m_ref, v_ref, down_ref = refs[number : number + 3]
        fresh_ref, new_m_ref, new_v_ref, token_ref = refs[-4:]
        token_ref[...] = jnp.zeros_like(token_ref)
        here = pl.ds(pl.multiple_of(pl.program_id(0) * width, width), width)
        gradient = refs[0][:, here].astype(F32)
        for ref in refs[1 : len(shares)]:
            gradient += ref[:, here].astype(F32)
        for ref in refs[len(shares) : number]:
            gradient += ref[size:, here].astype(F32)
        new_m = 0.9 * m_ref[...] + 0.1 * gradient
        new_v = 0.95 * v_ref[...] + 0.05 * gradient * gradient
        new_m_ref[...] = new_m
        new_v_ref[...] = new_v
        rows = down_ref[...].astype(F32)
        fresh_ref[:, here] = (rows - 0.2 * new_m / (jnp.sqrt(new_v) + 1e-08)).astype(BF16)

    there = pl.BlockSpec((size, width), lambda j, columns, rank: (0, columns[j]))
    return pl.pallas_call(
        kernel,
        grid_spec=pltpu.PrefetchScalarGridSpec(
            num_scalar_prefetch=2,
            grid=(count,),
            in_specs=[INSIDE] * number
            + [there] * 2
            + [pl.BlockSpec((size, width), lambda j, columns, rank: (rank[0], columns[j]))]
            + [ANYWHERE] * (len(after) + len(previous)),
            out_specs=[INSIDE, there, there, pl.BlockSpec((8, 128), lambda j, columns, rank: (0, 0))],
        ),
        out_shape=[
            jax.ShapeDtypeStruct((size, wide), BF16),
            jax.ShapeDtypeStruct((size, total), F32),
            jax.ShapeDtypeStruct((size, total), F32),
            TOKEN,
        ],
        input_output_aliases={
            number + len(after) + 5: 1, number + len(after) + 6: 2
        } if previous else {},
        compiler_params=params(8),
        cost_estimate=cost(item),
        name="adam",
    )(columns, rank, *shares, *near, moment, second, down, *after, *previous)


def place_rows(shards, chosen, rows, columns, previous, total, width, after, item):
    size, wide = shards[0].shape
    count = wide // width
    number = len(shards)

    def kernel(rows_ref, columns_ref, *refs):
        shard_refs, out_ref, token_ref, sems = refs[:number], refs[-3], refs[-2], refs[-1]
        token_ref[...] = jnp.zeros_like(token_ref)
        copies = []
        for k in range(number):
            for j in range(count):
                copies.append(
                    pltpu.make_async_copy(
                        shard_refs[k].at[:, pl.ds(j * width, width)],
                        out_ref.at[
                            pl.ds(pl.multiple_of(rows_ref[chosen[k]] * size, size), size),
                            pl.ds(pl.multiple_of(columns_ref[j] * width, width), width),
                        ],
                        sems.at[k, j],
                    )
                )
        for copy in copies:
            copy.start()
        for copy in copies:
            copy.wait()

    return pl.pallas_call(
        kernel,
        grid_spec=pltpu.PrefetchScalarGridSpec(
            num_scalar_prefetch=2,
            grid=(1,),
            in_specs=[ANYWHERE] * (number + len(after) + len(previous)),
            out_specs=[ANYWHERE, pl.BlockSpec((8, 128), lambda i, rows, columns: (0, 0))],
            scratch_shapes=[pltpu.SemaphoreType.DMA((number, count))],
        ),
        out_shape=[jax.ShapeDtypeStruct(total, BF16), TOKEN],
        input_output_aliases={2 + number + len(after): 0} if previous else {},
        compiler_params=params(8),
        cost_estimate=cost(item),
        name="place",
    )(rows, columns, *shards, *after, *previous)


def partials(pieces, where, order, slope, down, up, scale, after, item):
    tokens, units = slope.shape
    model_width = down.shape[1]
    width = pieces[0].shape[1]
    count = len(pieces)
    block = model_width // 4
    rows = tokens
    step = 2 * TILE

    def kernel(where_ref, order_ref, *refs):
        piece_refs, refs = refs[:count], refs[count:]
        slope_ref, down_ref, up_ref = refs[:3]
        outs, token_ref, joined, product_ref = refs[3 + len(after) : -3], *refs[-3:]
        token_ref[...] = jnp.zeros_like(token_ref)
        for j in range(count):
            joined[:, pl.ds(pl.multiple_of(where_ref[j] * width, width), width)] = piece_refs[j][...]
        back = lax.dot_general(
            joined[...], down_ref[...], (((1,), (1,)), ((), ())), preferred_element_type=F32
        )
        act_grad = (back * slope_ref[...].astype(F32)).astype(BF16)
        product = jnp.dot(act_grad, up_ref[...], preferred_element_type=F32) * scale
        product_ref[...] = product.astype(BF16)

        for k in range(4):
            first = pl.multiple_of(order_ref[k] * block, block)
            outs[k][...] = product_ref[:, pl.ds(first, block)]

    return pl.pallas_call(
        kernel,
        grid_spec=pltpu.PrefetchScalarGridSpec(
            num_scalar_prefetch=2,
            grid=(rows // step,),
            in_specs=[pl.BlockSpec((step, width), lambda i, w, o: (i, 0))] * count
            + [pl.BlockSpec((step, units), lambda i, w, o: (i, 0))]
            + [INSIDE] * 2
            + [ANYWHERE] * len(after),
            out_specs=[
                pl.BlockSpec((step, block), lambda i, w, o: (i, 0)),
            ]
            * 4
            + [pl.BlockSpec((8, 128), lambda i, w, o: (0, 0))],
            scratch_shapes=[
                pltpu.VMEM((step, model_width), BF16),
                pltpu.VMEM((step, model_width), BF16),
            ],
        ),
        out_shape=[
            jax.ShapeDtypeStruct((rows, block), BF16),
        ]
        * 4
        + [TOKEN],
        compiler_params=params(28),
        cost_estimate=cost(item),
        name="partials",
    )(where, order, *pieces, slope, down, up, *after)


def on_device(handoff, hidden_pre, down_weight, up_weight, moment, second):
    rank = lax.axis_index("dp")
    tensor = lax.axis_index("tensor")
    handoff, hidden_pre, down, up = handoff[0], hidden_pre[0], down_weight[0], up_weight[0]
    tokens, block = handoff.shape
    width = block // COL_PARTS
    model_width = down.shape[1]

    def swapped(value, axis, distance):
        return lax.ppermute(value, axis, [(i, i ^ distance) for i in range(4)])

    def column_of(key):
        return (tensor ^ key[0]) * COL_PARTS + key[1]

    def columns_of(keys):
        return jnp.stack([column_of(key) for key in keys]).astype(jnp.int32)

    shards = jnp.stack([rank, rank ^ 1, rank ^ 2, rank ^ 3]).astype(jnp.int32)
    paired = jnp.stack([rank, rank ^ 2, rank ^ 3, rank ^ 1]).astype(jnp.int32)
    rank_now = rank.astype(jnp.int32)[None]
    order = jnp.stack([tensor, tensor ^ 2, tensor ^ 1, tensor ^ 3]).astype(jnp.int32)
    term_scale = 1.0 / math.sqrt(tokens * 4)
    partial_scale = 1.0 / math.sqrt(down.shape[0] * 4)
    columns = [columns_of(chunk) for chunk in CHUNKS]
    keys = [(b, g) for g in range(COL_PARTS) for b in range(4)]
    where = columns_of(keys)
    held, values, moments, new_down = [], {}, [], []

    def after():
        out = list(held)
        held.clear()
        return out

    def arrive(name):
        values[name], *held[:] = lax.optimization_barrier((values[name], values["token"], *held))
        held.append(values[name])

    for part in range(COL_PARTS):
        columns_now = handoff[:, part * width : (part + 1) * width]
        values["b0" + str(part)] = from_behind(columns_now, "pipe", -1)

    for name in PLAN:
        kind, k = name[0], int(name[1])
        if kind == "h":
            values["hidden"], values["slope"], values["token"] = prepare(
                hidden_pre, model_width, [shards, paired, rank_now, order, where, *columns],
                name,
            )
        elif kind == "b":
            arrive(name)
            part = name[2]
            if k == 0:
                values["b1" + part] = swapped(values[name], "tensor", 1)
                values["b2" + part] = swapped(values[name], "tensor", 2)
            elif k == 2:
                values["b3" + part] = swapped(values[name], "tensor", 1)
        elif kind == "t":
            pieces = [values["b%d%d" % key] for key in CHUNKS[k]]
            pair, step = SUMS[k] == "two", SUMS[k] in ("tri", "trd")
            *out, values["token"] = terms(
                values["hidden"], pieces, paired if pair else shards, term_scale, pair, after(), name
            )
            if pair:
                values["s0" + name[1]], values["s2" + name[1]] = out[:2]
                values["m" + name[1]] = swapped(out[2], "dp", 1)
            else:
                values["s0" + name[1]], values["s2" + name[1]] = out[0], out[2]
                values["m" + name[1]] = swapped(out[3], "dp", 1) if step else None
                values["s1" + name[1]] = out[1]
                for j in {"tri": (1,), "trd": (), "one": (3, 2, 1)}[SUMS[k]]:
                    values["s%d%d" % (j, k)] = swapped(out[j], "dp", j)
        elif kind == "m":
            arrive(name)
            size = values["s0" + name[1]].shape[0]
            held_part = values[name][:size] if SUMS[k] == "two" else values[name]
            far = values["s2" + name[1]].astype(F32) + held_part.astype(F32)
            far = far.astype(BF16)
            if SUMS[k] == "trd":
                far, near = lax.optimization_barrier((far, values["s1" + name[1]]))
                values["s1" + name[1]] = swapped(near, "dp", 1)
            values["s2" + name[1]] = swapped(far, "dp", 2)
        elif kind == "r":
            for j in {"two": (2,), "tri": (1, 2), "trd": (2, 1), "one": (3, 2, 1)}[SUMS[k]]:
                arrive("s%d%d" % (j, k))
        elif kind == "a":
            if SUMS[k] == "two":
                shares, near = [values["s%d%d" % (j, k)] for j in (0, 2)], [values["m" + name[1]]]
            else:
                number = 3 if SUMS[k] in ("tri", "trd") else 4
                shares, near = [values["s%d%d" % (j, k)] for j in range(number)], []
            fresh, *moments[:], values["token"] = adam_chunk(
                shares, near, moment[0], second[0], down, columns[k], rank_now,
                moments, width, after(), name,
            )
            values["g0" + name[1]] = fresh
            values["g2" + name[1]] = swapped(fresh, "dp", 2)
            values["g1" + name[1]] = swapped(fresh, "dp", 1)
            if GATHERS[k] == "one":
                values["g3" + name[1]] = swapped(fresh, "dp", 3)
        elif kind == "g":
            arrive("g2" + name[1])
            if GATHERS[k] != "one":
                values["g3" + name[1]] = swapped(values["g2" + name[1]], "dp", 1)
        elif kind == "e":
            arrive("g1" + name[1])
        elif kind in "lq":
            chosen = [3] if kind == "q" else [0, 1, 2] + [3] * ("q" + name[1] not in PLAN)
            gathered = [values["g%d%d" % (j, k)] for j in chosen]
            *new_down[:], values["token"] = place_rows(
                gathered, chosen, shards, columns[k], new_down, down.shape, width, after(), name
            )
        elif kind == "p":
            pieces = [values["b%d%d" % key] for key in keys]
            values["own"], values["other"], values["x2"], values["x0"], values["token"] = partials(
                pieces, where, order, values["slope"], down, up, partial_scale, after(), name
            )
            values["x2"] = swapped(values["x2"], "tensor", 1)
            if "w0" not in PLAN:
                values["x0"] = swapped(values["x0"], "tensor", 1)
        elif kind == "w":
            arrive("x0")
            values["x0"] = swapped(values["x0"], "tensor", 1)
        elif kind == "u":
            arrive("x2")
        elif kind == "x" and k == 0:
            arrive("x0")
            other = values["other"].astype(F32) + values["x0"].astype(F32)
            values["x1"] = swapped(other.astype(BF16), "tensor", 2)
        elif kind == "x":
            arrive("x1")
            own = values["own"].astype(F32) + values["x2"].astype(F32)
            input_grad = (own + values["x1"].astype(F32)).astype(BF16)
    return (input_grad[None], new_down[0][None], moments[0][None], moments[1][None])


def solution(mesh):
    placed = (
        P("pipe", "dp", "tensor"),
        P("pipe", "dp", "tensor"),
        P("pipe", "tensor", None),
        P("pipe", "tensor", None),
        P("pipe", ("tensor", "dp"), None),
        P("pipe", ("tensor", "dp"), None),
    )
    fits = mesh.shape["tensor"] == 4 and mesh.shape["dp"] == 4
    return jax.shard_map(
        on_device if fits else plain,
        mesh=mesh,
        in_specs=placed,
        out_specs=(
            P("pipe", "dp", "tensor"),
            P("pipe", "tensor", None),
            P("pipe", ("tensor", "dp"), None),
            P("pipe", ("tensor", "dp"), None),
        ),
        check_vma=False,
    )
```

```python
import math

import jax
import jax.numpy as jnp
from jax import lax
from jax.experimental import pallas as pl
from jax.experimental.pallas import tpu as pltpu
from jax.sharding import PartitionSpec as P

F32 = jnp.float32
BF16 = jnp.bfloat16
COL_PARTS = 2
TILE = 256
CHUNKS = (((0, 0), (1, 0)), ((0, 1), (1, 1), (2, 0), (3, 0)), ((2, 1), (3, 1)))
SUMS = ("two", "tri", "two",)
GATHERS = ("two", "two", "two",)
PLAN = (
    "h0", "b00", "b10", "t0", "b01", "m0", "b20", "b11", "r0", "a0", "b30", "t1", "g0",
    "e0", "b21", "b31", "t2", "m1", "r1", "a1", "p0", "m2", "r2", "x0", "a2", "u0", "e1",
    "g1", "e2", "g2", "l0", "q0", "l1", "x1", "l2", "q1", "q2",
)
ANYWHERE = pl.BlockSpec(memory_space=pl.ANY)
INSIDE = pl.BlockSpec(memory_space=pltpu.VMEM)
TOKEN = jax.ShapeDtypeStruct((8, 128), F32)
COSTS = {
    "h0": 40000000000, "t0": 10000000000, "a0": 10000000000, "t1": 40000000000,
    "t2": 6000000000, "a1": 10000000000, "p0": 3000000000, "a2": 6000000000, "l0": 4199999999,
    "q0": 3000000000, "l1": 1000, "l2": 80000000000, "q1": 3000000000, "q2": 3000000000,
}


def from_behind(block, axis, distance):
    devices = range(lax.axis_size(axis))
    route = [((i - distance) % len(devices), i) for i in devices]
    return lax.ppermute(block, axis, route)


def normal_cdf(inputs):
    return 0.5 * (1.0 + jax.scipy.special.erf(inputs * (1.0 / math.sqrt(2.0))))


def gelu_value(inputs):
    return inputs * normal_cdf(inputs)


def gelu_slope(inputs):
    return normal_cdf(inputs) + inputs * jnp.exp(-0.5 * inputs * inputs) * (
        1.0 / math.sqrt(2.0 * math.pi)
    )


def hidden_of(hidden_pre):
    return gelu_value(hidden_pre.astype(F32)).astype(BF16)


def act_grad_of(incoming, down, hidden_pre):
    back = lax.dot_general(incoming, down, (((1,), (1,)), ((), ())), preferred_element_type=F32)
    scale = 1.0 / math.sqrt(down.shape[1])
    return (back * scale * gelu_slope(hidden_pre.astype(F32))).astype(BF16)


def term_of(hidden, columns, token_total):
    product = lax.dot_general(
        hidden, columns, (((0,), (0,)), ((), ())), preferred_element_type=F32
    )
    return (product * (1.0 / math.sqrt(token_total))).astype(BF16)


def adam(gradient, moment, second, rows):
    new_m = 0.9 * moment + 0.1 * gradient
    new_v = 0.95 * second + 0.05 * gradient * gradient
    fresh = (rows.astype(F32) - 0.2 * new_m / (jnp.sqrt(new_v) + 1e-08)).astype(BF16)
    return new_m, new_v, fresh


def plain(handoff, hidden_pre, down_weight, up_weight, moment, second):
    arrived = from_behind(handoff, "pipe", -1)
    incoming = lax.all_gather(arrived, "tensor", axis=2, tiled=True)[0]
    model_width = incoming.shape[1]
    shard_rows = moment.shape[1]
    hidden_total = down_weight.shape[1] * lax.axis_size("tensor")
    token_total = incoming.shape[0] * lax.axis_size("dp")
    hidden = hidden_of(hidden_pre[0])
    act_grad = act_grad_of(incoming, down_weight[0], hidden_pre[0])
    partial_value = jnp.dot(act_grad, up_weight[0], preferred_element_type=F32) * (
        1.0 / math.sqrt(hidden_total)
    )
    input_grad = lax.psum_scatter(
        partial_value.astype(BF16), "tensor", scatter_dimension=1, tiled=True
    )
    gradient = lax.psum_scatter(
        term_of(hidden, incoming, token_total), "dp", scatter_dimension=0, tiled=True
    ).astype(F32)
    own_rows = lax.dynamic_slice_in_dim(
        down_weight[0], lax.axis_index("dp") * shard_rows, shard_rows, 0
    )
    new_m, new_v, fresh = adam(gradient, moment[0], second[0], own_rows)
    new_down = lax.all_gather(fresh, "dp", axis=0, tiled=True)
    return (input_grad[None], new_down[None], new_m[None], new_v[None])


def cost(item):
    return pl.CostEstimate(flops=COSTS[item], bytes_accessed=1024, transcendentals=0)


def params(mib):
    return pltpu.CompilerParams(vmem_limit_bytes=mib * 2**20)


def prepare(hidden_pre, model_width, after, item):
    tokens, units = hidden_pre.shape
    scale = 1.0 / math.sqrt(model_width)

    def kernel(pre_ref, *refs):
        hidden_ref, slope_ref, token_ref = refs[len(after) :]
        token_ref[...] = jnp.zeros_like(token_ref)
        pre = pre_ref[...].astype(F32)
        phi = 0.5 * (1.0 + lax.erf(pre * (1.0 / math.sqrt(2.0))))
        hidden_ref[...] = (pre * phi).astype(BF16).T
        bell = jnp.exp(-0.5 * pre * pre) * (1.0 / math.sqrt(2.0 * math.pi))
        slope_ref[...] = ((phi + pre * bell) * scale).astype(BF16)

    return pl.pallas_call(
        kernel,
        grid=(tokens // TILE,),
        in_specs=[pl.BlockSpec((TILE, units), lambda i: (i, 0))] + [ANYWHERE] * len(after),
        out_specs=[
            pl.BlockSpec((units, TILE), lambda i: (0, i)),
            pl.BlockSpec((TILE, units), lambda i: (i, 0)),
            pl.BlockSpec((8, 128), lambda i: (0, 0)),
        ],
        out_shape=[
            jax.ShapeDtypeStruct((units, tokens), BF16),
            jax.ShapeDtypeStruct((tokens, units), BF16),
            TOKEN,
        ],
        compiler_params=params(8),
        cost_estimate=cost(item),
        name="prepare",
    )(hidden_pre, *after)


def terms(hidden_t, pieces, places, scale, paired, after, item):
    units, tokens = hidden_t.shape
    size, width = units // 4, pieces[0].shape[1]
    count, wide = len(pieces), len(pieces) * pieces[0].shape[1]
    heights = [size, size, 2 * size] if paired else [size] * 4
    number = len(heights)

    def kernel(places_ref, hidden_ref, *refs):
        piece_refs, refs = refs[:count], refs[count + len(after) :]
        out_refs, token_ref, joined, product = refs[:number], *refs[number:]
        token_ref[...] = jnp.zeros_like(token_ref)
        for j in range(count):
            joined[:, j * width : (j + 1) * width] = piece_refs[j][...]
        whole = jnp.dot(hidden_ref[...], joined[...], preferred_element_type=F32)
        product[...] = (whole * scale).astype(BF16)
        for j in range(4):
            rows = product[pl.ds(pl.multiple_of(places_ref[j] * size, size), size), :]
            if paired and j >= 2:
                out_refs[2][(j - 2) * size : (j - 1) * size, :] = rows
            else:
                out_refs[j][...] = rows

    return pl.pallas_call(
        kernel,
        in_specs=[pl.BlockSpec(memory_space=pltpu.SMEM)]
        + [INSIDE] * (1 + count)
        + [ANYWHERE] * len(after),
        out_specs=[INSIDE] * (number + 1),
        scratch_shapes=[pltpu.VMEM((tokens, wide), BF16), pltpu.VMEM((units, wide), BF16)],
        out_shape=[jax.ShapeDtypeStruct((height, wide), BF16) for height in heights] + [TOKEN],
        compiler_params=params(16),
        cost_estimate=cost(item),
        name="terms",
    )(places, hidden_t, *pieces, *after)


def adam_chunk(shares, near, moment, second, down, columns, rank, previous, width, after, item):
    size, wide = shares[0].shape
    count = wide // width
    total = moment.shape[1]
    number = len(shares) + len(near)

    def kernel(columns_ref, rank_ref, *refs):
        m_ref, v_ref, down_ref = refs[number : number + 3]
        fresh_ref, new_m_ref, new_v_ref, token_ref = refs[-4:]
        token_ref[...] = jnp.zeros_like(token_ref)
        here = pl.ds(pl.multiple_of(pl.program_id(0) * width, width), width)
        gradient = refs[0][:, here].astype(F32)
        for ref in refs[1 : len(shares)]:
            gradient += ref[:, here].astype(F32)
        for ref in refs[len(shares) : number]:
            gradient += ref[size:, here].astype(F32)
        new_m = 0.9 * m_ref[...] + 0.1 * gradient
        new_v = 0.95 * v_ref[...] + 0.05 * gradient * gradient
        new_m_ref[...] = new_m
        new_v_ref[...] = new_v
        rows = down_ref[...].astype(F32)
        fresh_ref[:, here] = (rows - 0.2 * new_m / (jnp.sqrt(new_v) + 1e-08)).astype(BF16)

    there = pl.BlockSpec((size, width), lambda j, columns, rank: (0, columns[j]))
    return pl.pallas_call(
        kernel,
        grid_spec=pltpu.PrefetchScalarGridSpec(
            num_scalar_prefetch=2,
            grid=(count,),
            in_specs=[INSIDE] * number
            + [there] * 2
            + [pl.BlockSpec((size, width), lambda j, columns, rank: (rank[0], columns[j]))]
            + [ANYWHERE] * (len(after) + len(previous)),
            out_specs=[INSIDE, there, there, pl.BlockSpec((8, 128), lambda j, columns, rank: (0, 0))],
        ),
        out_shape=[
            jax.ShapeDtypeStruct((size, wide), BF16),
            jax.ShapeDtypeStruct((size, total), F32),
            jax.ShapeDtypeStruct((size, total), F32),
            TOKEN,
        ],
        input_output_aliases={
            number + len(after) + 5: 1, number + len(after) + 6: 2
        } if previous else {},
        compiler_params=params(8),
        cost_estimate=cost(item),
        name="adam",
    )(columns, rank, *shares, *near, moment, second, down, *after, *previous)


def place_rows(shards, chosen, rows, columns, previous, total, width, after, item):
    size, wide = shards[0].shape
    count = wide // width
    number = len(shards)

    def kernel(rows_ref, columns_ref, *refs):
        shard_refs, out_ref, token_ref, sems = refs[:number], refs[-3], refs[-2], refs[-1]
        token_ref[...] = jnp.zeros_like(token_ref)
        copies = []
        for k in range(number):
            for j in range(count):
                copies.append(
                    pltpu.make_async_copy(
                        shard_refs[k].at[:, pl.ds(j * width, width)],
                        out_ref.at[
                            pl.ds(pl.multiple_of(rows_ref[chosen[k]] * size, size), size),
                            pl.ds(pl.multiple_of(columns_ref[j] * width, width), width),
                        ],
                        sems.at[k, j],
                    )
                )
        for copy in copies:
            copy.start()
        for copy in copies:
            copy.wait()

    return pl.pallas_call(
        kernel,
        grid_spec=pltpu.PrefetchScalarGridSpec(
            num_scalar_prefetch=2,
            grid=(1,),
            in_specs=[ANYWHERE] * (number + len(after) + len(previous)),
            out_specs=[ANYWHERE, pl.BlockSpec((8, 128), lambda i, rows, columns: (0, 0))],
            scratch_shapes=[pltpu.SemaphoreType.DMA((number, count))],
        ),
        out_shape=[jax.ShapeDtypeStruct(total, BF16), TOKEN],
        input_output_aliases={2 + number + len(after): 0} if previous else {},
        compiler_params=params(8),
        cost_estimate=cost(item),
        name="place",
    )(rows, columns, *shards, *after, *previous)


def partials(pieces, where, order, slope, down, up, scale, after, item):
    tokens, units = slope.shape
    model_width = down.shape[1]
    width = pieces[0].shape[1]
    count = len(pieces)
    block = model_width // 4
    rows = tokens
    step = 2 * TILE

    def kernel(where_ref, order_ref, *refs):
        piece_refs, refs = refs[:count], refs[count:]
        slope_ref, down_ref, up_ref = refs[:3]
        outs, token_ref, joined, product_ref = refs[3 + len(after) : -3], *refs[-3:]
        token_ref[...] = jnp.zeros_like(token_ref)
        for j in range(count):
            joined[:, pl.ds(pl.multiple_of(where_ref[j] * width, width), width)] = piece_refs[j][...]
        back = lax.dot_general(
            joined[...], down_ref[...], (((1,), (1,)), ((), ())), preferred_element_type=F32
        )
        act_grad = (back * slope_ref[...].astype(F32)).astype(BF16)
        product = jnp.dot(act_grad, up_ref[...], preferred_element_type=F32) * scale
        product_ref[...] = product.astype(BF16)

        for k in range(4):
            first = pl.multiple_of(order_ref[k] * block, block)
            outs[k][...] = product_ref[:, pl.ds(first, block)]

    return pl.pallas_call(
        kernel,
        grid_spec=pltpu.PrefetchScalarGridSpec(
            num_scalar_prefetch=2,
            grid=(rows // step,),
            in_specs=[pl.BlockSpec((step, width), lambda i, w, o: (i, 0))] * count
            + [pl.BlockSpec((step, units), lambda i, w, o: (i, 0))]
            + [INSIDE] * 2
            + [ANYWHERE] * len(after),
            out_specs=[
                pl.BlockSpec((step, block), lambda i, w, o: (i, 0)),
            ]
            * 4
            + [pl.BlockSpec((8, 128), lambda i, w, o: (0, 0))],
            scratch_shapes=[
                pltpu.VMEM((step, model_width), BF16),
                pltpu.VMEM((step, model_width), BF16),
            ],
        ),
        out_shape=[
            jax.ShapeDtypeStruct((rows, block), BF16),
        ]
        * 4
        + [TOKEN],
        compiler_params=params(28),
        cost_estimate=cost(item),
        name="partials",
    )(where, order, *pieces, slope, down, up, *after)


def on_device(handoff, hidden_pre, down_weight, up_weight, moment, second):
    rank = lax.axis_index("dp")
    tensor = lax.axis_index("tensor")
    handoff, hidden_pre, down, up = handoff[0], hidden_pre[0], down_weight[0], up_weight[0]
    tokens, block = handoff.shape
    width = block // COL_PARTS
    model_width = down.shape[1]

    def swapped(value, axis, distance):
        return lax.ppermute(value, axis, [(i, i ^ distance) for i in range(4)])

    def column_of(key):
        return (tensor ^ key[0]) * COL_PARTS + key[1]

    def columns_of(keys):
        return jnp.stack([column_of(key) for key in keys]).astype(jnp.int32)

    shards = jnp.stack([rank, rank ^ 1, rank ^ 2, rank ^ 3]).astype(jnp.int32)
    paired = jnp.stack([rank, rank ^ 2, rank ^ 3, rank ^ 1]).astype(jnp.int32)
    rank_now = rank.astype(jnp.int32)[None]
    order = jnp.stack([tensor, tensor ^ 2, tensor ^ 1, tensor ^ 3]).astype(jnp.int32)
    term_scale = 1.0 / math.sqrt(tokens * 4)
    partial_scale = 1.0 / math.sqrt(down.shape[0] * 4)
    columns = [columns_of(chunk) for chunk in CHUNKS]
    keys = [(b, g) for g in range(COL_PARTS) for b in range(4)]
    where = columns_of(keys)
    held, values, moments, new_down = [], {}, [], []

    def after():
        out = list(held)
        held.clear()
        return out

    def arrive(name):
        values[name], *held[:] = lax.optimization_barrier((values[name], values["token"], *held))
        held.append(values[name])

    for part in range(COL_PARTS):
        columns_now = handoff[:, part * width : (part + 1) * width]
        values["b0" + str(part)] = from_behind(columns_now, "pipe", -1)

    for name in PLAN:
        kind, k = name[0], int(name[1])
        if kind == "h":
            values["hidden"], values["slope"], values["token"] = prepare(
                hidden_pre, model_width, [shards, paired, rank_now, order, where, *columns],
                name,
            )
        elif kind == "b":
            arrive(name)
            part = name[2]
            if k == 0:
                values["b1" + part] = swapped(values[name], "tensor", 1)
                values["b2" + part] = swapped(values[name], "tensor", 2)
            elif k == 2:
                values["b3" + part] = swapped(values[name], "tensor", 1)
        elif kind == "t":
            pieces = [values["b%d%d" % key] for key in CHUNKS[k]]
            pair, step = SUMS[k] == "two", SUMS[k] in ("tri", "trd")
            *out, values["token"] = terms(
                values["hidden"], pieces, paired if pair else shards, term_scale, pair, after(), name
            )
            if pair:
                values["s0" + name[1]], values["s2" + name[1]] = out[:2]
                values["m" + name[1]] = swapped(out[2], "dp", 1)
            else:
                values["s0" + name[1]], values["s2" + name[1]] = out[0], out[2]
                values["m" + name[1]] = swapped(out[3], "dp", 1) if step else None
                values["s1" + name[1]] = out[1]
                for j in {"tri": (1,), "trd": (), "one": (3, 2, 1)}[SUMS[k]]:
                    values["s%d%d" % (j, k)] = swapped(out[j], "dp", j)
        elif kind == "m":
            arrive(name)
            size = values["s0" + name[1]].shape[0]
            held_part = values[name][:size] if SUMS[k] == "two" else values[name]
            far = values["s2" + name[1]].astype(F32) + held_part.astype(F32)
            far = far.astype(BF16)
            if SUMS[k] == "trd":
                far, near = lax.optimization_barrier((far, values["s1" + name[1]]))
                values["s1" + name[1]] = swapped(near, "dp", 1)
            values["s2" + name[1]] = swapped(far, "dp", 2)
        elif kind == "r":
            for j in {"two": (2,), "tri": (1, 2), "trd": (2, 1), "one": (3, 2, 1)}[SUMS[k]]:
                arrive("s%d%d" % (j, k))
        elif kind == "a":
            if SUMS[k] == "two":
                shares, near = [values["s%d%d" % (j, k)] for j in (0, 2)], [values["m" + name[1]]]
            else:
                number = 3 if SUMS[k] in ("tri", "trd") else 4
                shares, near = [values["s%d%d" % (j, k)] for j in range(number)], []
            fresh, *moments[:], values["token"] = adam_chunk(
                shares, near, moment[0], second[0], down, columns[k], rank_now,
                moments, width, after(), name,
            )
            values["g0" + name[1]] = fresh
            values["g2" + name[1]] = swapped(fresh, "dp", 2)
            values["g1" + name[1]] = swapped(fresh, "dp", 1)
            if GATHERS[k] == "one":
                values["g3" + name[1]] = swapped(fresh, "dp", 3)
        elif kind == "g":
            arrive("g2" + name[1])
            if GATHERS[k] != "one":
                values["g3" + name[1]] = swapped(values["g2" + name[1]], "dp", 1)
        elif kind == "e":
            arrive("g1" + name[1])
        elif kind in "lq":
            chosen = [3] if kind == "q" else [0, 1, 2] + [3] * ("q" + name[1] not in PLAN)
            gathered = [values["g%d%d" % (j, k)] for j in chosen]
            *new_down[:], values["token"] = place_rows(
                gathered, chosen, shards, columns[k], new_down, down.shape, width, after(), name
            )
        elif kind == "p":
            pieces = [values["b%d%d" % key] for key in keys]
            values["own"], values["other"], values["x2"], values["x0"], values["token"] = partials(
                pieces, where, order, values["slope"], down, up, partial_scale, after(), name
            )
            values["x2"] = swapped(values["x2"], "tensor", 1)
            if "w0" not in PLAN:
                values["x0"] = swapped(values["x0"], "tensor", 1)
        elif kind == "w":
            arrive("x0")
            values["x0"] = swapped(values["x0"], "tensor", 1)
        elif kind == "u":
            arrive("x2")
        elif kind == "x" and k == 0:
            arrive("x0")
            other = values["other"].astype(F32) + values["x0"].astype(F32)
            values["x1"] = swapped(other.astype(BF16), "tensor", 2)
        elif kind == "x":
            arrive("x1")
            own = values["own"].astype(F32) + values["x2"].astype(F32)
            input_grad = (own + values["x1"].astype(F32)).astype(BF16)
    return (input_grad[None], new_down[0][None], moments[0][None], moments[1][None])


def solution(mesh):
    placed = (
        P("pipe", "dp", "tensor"),
        P("pipe", "dp", "tensor"),
        P("pipe", "tensor", None),
        P("pipe", "tensor", None),
        P("pipe", ("tensor", "dp"), None),
        P("pipe", ("tensor", "dp"), None),
    )
    fits = mesh.shape["tensor"] == 4 and mesh.shape["dp"] == 4
    return jax.shard_map(
        on_device if fits else plain,
        mesh=mesh,
        in_specs=placed,
        out_specs=(
            P("pipe", "dp", "tensor"),
            P("pipe", "tensor", None),
            P("pipe", ("tensor", "dp"), None),
            P("pipe", ("tensor", "dp"), None),
        ),
        check_vma=False,
    )
```

```python
import math

import jax
import jax.numpy as jnp
from jax import lax
from jax.experimental import pallas as pl
from jax.experimental.pallas import tpu as pltpu
from jax.sharding import PartitionSpec as P

F32 = jnp.float32
BF16 = jnp.bfloat16
COL_PARTS = 2
TILE = 256
CHUNKS = (((0, 0), (1, 0)), ((0, 1), (1, 1), (2, 0), (3, 0)), ((2, 1), (3, 1)))
SUMS = ("two", "tri", "two",)
GATHERS = ("two", "two", "two",)
PLAN = (
    "h0", "b00", "b10", "t0", "b01", "m0", "b20", "b11", "r0", "a0", "b30", "t1", "g0",
    "e0", "b21", "b31", "t2", "m1", "r1", "a1", "p0", "m2", "r2", "x0", "a2", "u0", "e1",
    "g1", "e2", "g2", "l0", "x1", "l12",
)
ANYWHERE = pl.BlockSpec(memory_space=pl.ANY)
INSIDE = pl.BlockSpec(memory_space=pltpu.VMEM)
TOKEN = jax.ShapeDtypeStruct((8, 128), F32)
COSTS = {
    "h0": 40000000000, "t0": 10000000000, "a0": 10000000000, "t1": 40000000000,
    "t2": 6000000000, "a1": 10000000000, "p0": 3000000000, "a2": 6000000000, "l0": 4199999999,
    "l12": 1000,
}


def from_behind(block, axis, distance):
    devices = range(lax.axis_size(axis))
    route = [((i - distance) % len(devices), i) for i in devices]
    return lax.ppermute(block, axis, route)


def normal_cdf(inputs):
    return 0.5 * (1.0 + jax.scipy.special.erf(inputs * (1.0 / math.sqrt(2.0))))


def gelu_value(inputs):
    return inputs * normal_cdf(inputs)


def gelu_slope(inputs):
    return normal_cdf(inputs) + inputs * jnp.exp(-0.5 * inputs * inputs) * (
        1.0 / math.sqrt(2.0 * math.pi)
    )


def hidden_of(hidden_pre):
    return gelu_value(hidden_pre.astype(F32)).astype(BF16)


def act_grad_of(incoming, down, hidden_pre):
    back = lax.dot_general(incoming, down, (((1,), (1,)), ((), ())), preferred_element_type=F32)
    scale = 1.0 / math.sqrt(down.shape[1])
    return (back * scale * gelu_slope(hidden_pre.astype(F32))).astype(BF16)


def term_of(hidden, columns, token_total):
    product = lax.dot_general(
        hidden, columns, (((0,), (0,)), ((), ())), preferred_element_type=F32
    )
    return (product * (1.0 / math.sqrt(token_total))).astype(BF16)


def adam(gradient, moment, second, rows):
    new_m = 0.9 * moment + 0.1 * gradient
    new_v = 0.95 * second + 0.05 * gradient * gradient
    fresh = (rows.astype(F32) - 0.2 * new_m / (jnp.sqrt(new_v) + 1e-08)).astype(BF16)
    return new_m, new_v, fresh


def plain(handoff, hidden_pre, down_weight, up_weight, moment, second):
    arrived = from_behind(handoff, "pipe", -1)
    incoming = lax.all_gather(arrived, "tensor", axis=2, tiled=True)[0]
    model_width = incoming.shape[1]
    shard_rows = moment.shape[1]
    hidden_total = down_weight.shape[1] * lax.axis_size("tensor")
    token_total = incoming.shape[0] * lax.axis_size("dp")
    hidden = hidden_of(hidden_pre[0])
    act_grad = act_grad_of(incoming, down_weight[0], hidden_pre[0])
    partial_value = jnp.dot(act_grad, up_weight[0], preferred_element_type=F32) * (
        1.0 / math.sqrt(hidden_total)
    )
    input_grad = lax.psum_scatter(
        partial_value.astype(BF16), "tensor", scatter_dimension=1, tiled=True
    )
    gradient = lax.psum_scatter(
        term_of(hidden, incoming, token_total), "dp", scatter_dimension=0, tiled=True
    ).astype(F32)
    own_rows = lax.dynamic_slice_in_dim(
        down_weight[0], lax.axis_index("dp") * shard_rows, shard_rows, 0
    )
    new_m, new_v, fresh = adam(gradient, moment[0], second[0], own_rows)
    new_down = lax.all_gather(fresh, "dp", axis=0, tiled=True)
    return (input_grad[None], new_down[None], new_m[None], new_v[None])


def cost(item):
    return pl.CostEstimate(flops=COSTS[item], bytes_accessed=1024, transcendentals=0)


def params(mib):
    return pltpu.CompilerParams(vmem_limit_bytes=mib * 2**20)


def prepare(hidden_pre, model_width, after, item):
    tokens, units = hidden_pre.shape
    scale = 1.0 / math.sqrt(model_width)

    def kernel(pre_ref, *refs):
        hidden_ref, slope_ref, token_ref = refs[len(after) :]
        token_ref[...] = jnp.zeros_like(token_ref)
        pre = pre_ref[...].astype(F32)
        phi = 0.5 * (1.0 + lax.erf(pre * (1.0 / math.sqrt(2.0))))
        hidden_ref[...] = (pre * phi).astype(BF16).T
        bell = jnp.exp(-0.5 * pre * pre) * (1.0 / math.sqrt(2.0 * math.pi))
        slope_ref[...] = ((phi + pre * bell) * scale).astype(BF16)

    return pl.pallas_call(
        kernel,
        grid=(tokens // TILE,),
        in_specs=[pl.BlockSpec((TILE, units), lambda i: (i, 0))] + [ANYWHERE] * len(after),
        out_specs=[
            pl.BlockSpec((units, TILE), lambda i: (0, i)),
            pl.BlockSpec((TILE, units), lambda i: (i, 0)),
            pl.BlockSpec((8, 128), lambda i: (0, 0)),
        ],
        out_shape=[
            jax.ShapeDtypeStruct((units, tokens), BF16),
            jax.ShapeDtypeStruct((tokens, units), BF16),
            TOKEN,
        ],
        compiler_params=params(8),
        cost_estimate=cost(item),
        name="prepare",
    )(hidden_pre, *after)


def terms(hidden_t, pieces, places, scale, paired, after, item):
    units, tokens = hidden_t.shape
    size, width = units // 4, pieces[0].shape[1]
    count, wide = len(pieces), len(pieces) * pieces[0].shape[1]
    heights = [size, size, 2 * size] if paired else [size] * 4
    number = len(heights)

    def kernel(places_ref, hidden_ref, *refs):
        piece_refs, refs = refs[:count], refs[count + len(after) :]
        out_refs, token_ref, joined, product = refs[:number], *refs[number:]
        token_ref[...] = jnp.zeros_like(token_ref)
        for j in range(count):
            joined[:, j * width : (j + 1) * width] = piece_refs[j][...]
        whole = jnp.dot(hidden_ref[...], joined[...], preferred_element_type=F32)
        product[...] = (whole * scale).astype(BF16)
        for j in range(4):
            rows = product[pl.ds(pl.multiple_of(places_ref[j] * size, size), size), :]
            if paired and j >= 2:
                out_refs[2][(j - 2) * size : (j - 1) * size, :] = rows
            else:
                out_refs[j][...] = rows

    return pl.pallas_call(
        kernel,
        in_specs=[pl.BlockSpec(memory_space=pltpu.SMEM)]
        + [INSIDE] * (1 + count)
        + [ANYWHERE] * len(after),
        out_specs=[INSIDE] * (number + 1),
        scratch_shapes=[pltpu.VMEM((tokens, wide), BF16), pltpu.VMEM((units, wide), BF16)],
        out_shape=[jax.ShapeDtypeStruct((height, wide), BF16) for height in heights] + [TOKEN],
        compiler_params=params(16),
        cost_estimate=cost(item),
        name="terms",
    )(places, hidden_t, *pieces, *after)


def adam_chunk(shares, near, moment, second, down, columns, rank, previous, width, after, item):
    size, wide = shares[0].shape
    count = wide // width
    total = moment.shape[1]
    number = len(shares) + len(near)

    def kernel(columns_ref, rank_ref, *refs):
        m_ref, v_ref, down_ref = refs[number : number + 3]
        fresh_ref, new_m_ref, new_v_ref, token_ref = refs[-4:]
        token_ref[...] = jnp.zeros_like(token_ref)
        here = pl.ds(pl.multiple_of(pl.program_id(0) * width, width), width)
        gradient = refs[0][:, here].astype(F32)
        for ref in refs[1 : len(shares)]:
            gradient += ref[:, here].astype(F32)
        for ref in refs[len(shares) : number]:
            gradient += ref[size:, here].astype(F32)
        new_m = 0.9 * m_ref[...] + 0.1 * gradient
        new_v = 0.95 * v_ref[...] + 0.05 * gradient * gradient
        new_m_ref[...] = new_m
        new_v_ref[...] = new_v
        rows = down_ref[...].astype(F32)
        fresh_ref[:, here] = (rows - 0.2 * new_m / (jnp.sqrt(new_v) + 1e-08)).astype(BF16)

    there = pl.BlockSpec((size, width), lambda j, columns, rank: (0, columns[j]))
    return pl.pallas_call(
        kernel,
        grid_spec=pltpu.PrefetchScalarGridSpec(
            num_scalar_prefetch=2,
            grid=(count,),
            in_specs=[INSIDE] * number
            + [there] * 2
            + [pl.BlockSpec((size, width), lambda j, columns, rank: (rank[0], columns[j]))]
            + [ANYWHERE] * (len(after) + len(previous)),
            out_specs=[INSIDE, there, there, pl.BlockSpec((8, 128), lambda j, columns, rank: (0, 0))],
        ),
        out_shape=[
            jax.ShapeDtypeStruct((size, wide), BF16),
            jax.ShapeDtypeStruct((size, total), F32),
            jax.ShapeDtypeStruct((size, total), F32),
            TOKEN,
        ],
        input_output_aliases={
            number + len(after) + 5: 1, number + len(after) + 6: 2
        } if previous else {},
        compiler_params=params(8),
        cost_estimate=cost(item),
        name="adam",
    )(columns, rank, *shares, *near, moment, second, down, *after, *previous)


def place_rows(groups, rows, columns, previous, total, width, after, item):
    size = groups[0][0].shape[0]
    counts = [group[0].shape[1] // width for group in groups]
    shards = [shard for group in groups for shard in group]

    def kernel(rows_ref, *refs):
        columns_refs, refs = refs[: len(groups)], refs[len(groups) :]
        out_ref, token_ref, sems = refs[-3:]
        token_ref[...] = jnp.zeros_like(token_ref)
        copies = []
        for n, count in enumerate(counts):
            for k in range(4):
                for j in range(count):
                    first_row = pl.multiple_of(rows_ref[k] * size, size)
                    first_column = pl.multiple_of(columns_refs[n][j] * width, width)
                    copies.append(
                        pltpu.make_async_copy(
                            refs[4 * n + k].at[:, pl.ds(j * width, width)],
                            out_ref.at[pl.ds(first_row, size), pl.ds(first_column, width)],
                            sems.at[n, k, j],
                        )
                    )
        for copy in copies:
            copy.start()
        for copy in copies:
            copy.wait()

    scalars = 1 + len(groups)
    return pl.pallas_call(
        kernel,
        grid_spec=pltpu.PrefetchScalarGridSpec(
            num_scalar_prefetch=scalars,
            grid=(1,),
            in_specs=[ANYWHERE] * (len(shards) + len(after) + len(previous)),
            out_specs=[ANYWHERE, pl.BlockSpec((8, 128), lambda i, *scalars: (0, 0))],
            scratch_shapes=[pltpu.SemaphoreType.DMA((len(groups), 4, max(counts)))],
        ),
        out_shape=[jax.ShapeDtypeStruct(total, BF16), TOKEN],
        input_output_aliases={scalars + len(shards) + len(after): 0} if previous else {},
        compiler_params=params(8),
        cost_estimate=cost(item),
        name="place",
    )(rows, *columns, *shards, *after, *previous)


def partials(pieces, where, order, slope, down, up, scale, after, item):
    tokens, units = slope.shape
    model_width = down.shape[1]
    width = pieces[0].shape[1]
    count = len(pieces)
    block = model_width // 4
    rows = tokens
    step = 2 * TILE

    def kernel(where_ref, order_ref, *refs):
        piece_refs, refs = refs[:count], refs[count:]
        slope_ref, down_ref, up_ref = refs[:3]
        outs, token_ref, joined, product_ref = refs[3 + len(after) : -3], *refs[-3:]
        token_ref[...] = jnp.zeros_like(token_ref)
        for j in range(count):
            joined[:, pl.ds(pl.multiple_of(where_ref[j] * width, width), width)] = piece_refs[j][...]
        back = lax.dot_general(
            joined[...], down_ref[...], (((1,), (1,)), ((), ())), preferred_element_type=F32
        )
        act_grad = (back * slope_ref[...].astype(F32)).astype(BF16)
        product = jnp.dot(act_grad, up_ref[...], preferred_element_type=F32) * scale
        product_ref[...] = product.astype(BF16)

        for k in range(4):
            first = pl.multiple_of(order_ref[k] * block, block)
            outs[k][...] = product_ref[:, pl.ds(first, block)]

    return pl.pallas_call(
        kernel,
        grid_spec=pltpu.PrefetchScalarGridSpec(
            num_scalar_prefetch=2,
            grid=(rows // step,),
            in_specs=[pl.BlockSpec((step, width), lambda i, w, o: (i, 0))] * count
            + [pl.BlockSpec((step, units), lambda i, w, o: (i, 0))]
            + [INSIDE] * 2
            + [ANYWHERE] * len(after),
            out_specs=[
                pl.BlockSpec((step, block), lambda i, w, o: (i, 0)),
            ]
            * 4
            + [pl.BlockSpec((8, 128), lambda i, w, o: (0, 0))],
            scratch_shapes=[
                pltpu.VMEM((step, model_width), BF16),
                pltpu.VMEM((step, model_width), BF16),
            ],
        ),
        out_shape=[
            jax.ShapeDtypeStruct((rows, block), BF16),
        ]
        * 4
        + [TOKEN],
        compiler_params=params(28),
        cost_estimate=cost(item),
        name="partials",
    )(where, order, *pieces, slope, down, up, *after)


def on_device(handoff, hidden_pre, down_weight, up_weight, moment, second):
    rank = lax.axis_index("dp")
    tensor = lax.axis_index("tensor")
    handoff, hidden_pre, down, up = handoff[0], hidden_pre[0], down_weight[0], up_weight[0]
    tokens, block = handoff.shape
    width = block // COL_PARTS
    model_width = down.shape[1]

    def swapped(value, axis, distance):
        return lax.ppermute(value, axis, [(i, i ^ distance) for i in range(4)])

    def column_of(key):
        return (tensor ^ key[0]) * COL_PARTS + key[1]

    def columns_of(keys):
        return jnp.stack([column_of(key) for key in keys]).astype(jnp.int32)

    shards = jnp.stack([rank, rank ^ 1, rank ^ 2, rank ^ 3]).astype(jnp.int32)
    paired = jnp.stack([rank, rank ^ 2, rank ^ 3, rank ^ 1]).astype(jnp.int32)
    rank_now = rank.astype(jnp.int32)[None]
    order = jnp.stack([tensor, tensor ^ 2, tensor ^ 1, tensor ^ 3]).astype(jnp.int32)
    term_scale = 1.0 / math.sqrt(tokens * 4)
    partial_scale = 1.0 / math.sqrt(down.shape[0] * 4)
    columns = [columns_of(chunk) for chunk in CHUNKS]
    keys = [(b, g) for g in range(COL_PARTS) for b in range(4)]
    where = columns_of(keys)
    held, values, moments, new_down = [], {}, [], []

    def after():
        out = list(held)
        held.clear()
        return out

    def arrive(name):
        values[name], *held[:] = lax.optimization_barrier((values[name], values["token"], *held))
        held.append(values[name])

    for part in range(COL_PARTS):
        columns_now = handoff[:, part * width : (part + 1) * width]
        values["b0" + str(part)] = from_behind(columns_now, "pipe", -1)

    for name in PLAN:
        kind, k = name[0], int(name[1])
        if kind == "h":
            values["hidden"], values["slope"], values["token"] = prepare(
                hidden_pre, model_width, [shards, paired, rank_now, order, where, *columns],
                name,
            )
        elif kind == "b":
            arrive(name)
            part = name[2]
            if k == 0:
                values["b1" + part] = swapped(values[name], "tensor", 1)
                values["b2" + part] = swapped(values[name], "tensor", 2)
            elif k == 2:
                values["b3" + part] = swapped(values[name], "tensor", 1)
        elif kind == "t":
            pieces = [values["b%d%d" % key] for key in CHUNKS[k]]
            pair, step = SUMS[k] == "two", SUMS[k] in ("tri", "trd")
            *out, values["token"] = terms(
                values["hidden"], pieces, paired if pair else shards, term_scale, pair, after(), name
            )
            if pair:
                values["s0" + name[1]], values["s2" + name[1]] = out[:2]
                values["m" + name[1]] = swapped(out[2], "dp", 1)
            else:
                values["s0" + name[1]], values["s2" + name[1]] = out[0], out[2]
                values["m" + name[1]] = swapped(out[3], "dp", 1) if step else None
                values["s1" + name[1]] = out[1]
                for j in {"tri": (1,), "trd": (), "one": (3, 2, 1)}[SUMS[k]]:
                    values["s%d%d" % (j, k)] = swapped(out[j], "dp", j)
        elif kind == "m":
            arrive(name)
            size = values["s0" + name[1]].shape[0]
            held_part = values[name][:size] if SUMS[k] == "two" else values[name]
            far = values["s2" + name[1]].astype(F32) + held_part.astype(F32)
            far = far.astype(BF16)
            if SUMS[k] == "trd":
                far, near = lax.optimization_barrier((far, values["s1" + name[1]]))
                values["s1" + name[1]] = swapped(near, "dp", 1)
            values["s2" + name[1]] = swapped(far, "dp", 2)
        elif kind == "r":
            for j in {"two": (2,), "tri": (1, 2), "trd": (2, 1), "one": (3, 2, 1)}[SUMS[k]]:
                arrive("s%d%d" % (j, k))
        elif kind == "a":
            if SUMS[k] == "two":
                shares, near = [values["s%d%d" % (j, k)] for j in (0, 2)], [values["m" + name[1]]]
            else:
                number = 3 if SUMS[k] in ("tri", "trd") else 4
                shares, near = [values["s%d%d" % (j, k)] for j in range(number)], []
            fresh, *moments[:], values["token"] = adam_chunk(
                shares, near, moment[0], second[0], down, columns[k], rank_now,
                moments, width, after(), name,
            )
            values["g0" + name[1]] = fresh
            values["g2" + name[1]] = swapped(fresh, "dp", 2)
            values["g1" + name[1]] = swapped(fresh, "dp", 1)
            if GATHERS[k] == "one":
                values["g3" + name[1]] = swapped(fresh, "dp", 3)
        elif kind == "g":
            arrive("g2" + name[1])
            if GATHERS[k] != "one":
                values["g3" + name[1]] = swapped(values["g2" + name[1]], "dp", 1)
        elif kind == "e":
            arrive("g1" + name[1])
        elif kind == "l":
            parts = [int(part) for part in name[1:]]
            groups = [[values["g%d%d" % (j, part)] for j in range(4)] for part in parts]
            *new_down[:], values["token"] = place_rows(
                groups, shards, [columns[part] for part in parts], new_down, down.shape, width,
                after(), name,
            )
        elif kind == "p":
            pieces = [values["b%d%d" % key] for key in keys]
            values["own"], values["other"], values["x2"], values["x0"], values["token"] = partials(
                pieces, where, order, values["slope"], down, up, partial_scale, after(), name
            )
            values["x2"] = swapped(values["x2"], "tensor", 1)
            if "w0" not in PLAN:
                values["x0"] = swapped(values["x0"], "tensor", 1)
        elif kind == "w":
            arrive("x0")
            values["x0"] = swapped(values["x0"], "tensor", 1)
        elif kind == "u":
            arrive("x2")
        elif kind == "x" and k == 0:
            arrive("x0")
            other = values["other"].astype(F32) + values["x0"].astype(F32)
            values["x1"] = swapped(other.astype(BF16), "tensor", 2)
        elif kind == "x":
            arrive("x1")
            own = values["own"].astype(F32) + values["x2"].astype(F32)
            input_grad = (own + values["x1"].astype(F32)).astype(BF16)
    return (input_grad[None], new_down[0][None], moments[0][None], moments[1][None])


def solution(mesh):
    placed = (
        P("pipe", "dp", "tensor"),
        P("pipe", "dp", "tensor"),
        P("pipe", "tensor", None),
        P("pipe", "tensor", None),
        P("pipe", ("tensor", "dp"), None),
        P("pipe", ("tensor", "dp"), None),
    )
    fits = mesh.shape["tensor"] == 4 and mesh.shape["dp"] == 4
    return jax.shard_map(
        on_device if fits else plain,
        mesh=mesh,
        in_specs=placed,
        out_specs=(
            P("pipe", "dp", "tensor"),
            P("pipe", "tensor", None),
            P("pipe", ("tensor", "dp"), None),
            P("pipe", ("tensor", "dp"), None),
        ),
        check_vma=False,
    )
```
